128 devices in a mesh: orb: 16 (over z, y_lo, core), aux: 8 (over y_hi, x).
Axes of the slice: x: 4, y: 4 (y_hi: 2, y_lo: 2; y = y_hi * 2 + y_lo), z: 4, core: 2. Of those that a mesh axis runs over, the one named last changes fastest.
Arguments:
- three_center: bfloat16 [512, 128, 128, 128], P(('orb', 'aux')), may hold values from -0.5 to 0.5
- screening: int32 [512, 3], P(('orb', 'aux')), may hold values from -1 to 511, as said below
- density_factor: bfloat16 [65536, 128], P('orb'), may hold values from -0.23925781 to 0.23925781
- metric_inverse: bfloat16 [1024, 1024], replicated, may hold values from -1 to 1, as said below
Outputs:
- exchange_block: bfloat16 [2048, 256], P('orb')
The draws below stay inside these ranges and needn't reach their ends.
Inputs may be any that keep to these rules, and one draw needn't show every extreme that they name: `screening`: A device's slots are 4 consecutive rows, devices in order of orb index then aux index. Column 0 equals the orb index and column 2 the aux index of the device holding the row. Column 1 is an orbital block, or -1 for an empty slot; empty slots follow the live ones, the live orbital blocks of a device are distinct, every device has 1 to 4 live slots, and some device has 4. `metric_inverse`: Symmetric.
All inputs are finite; a program needn't handle non-finite values.
Results may differ from the reference program's by a relative error of at most 0.0063.
Values may be sent and summed in bfloat16 or wider, within the bound.
A program may use at most 128 MiB of HBM per device.

```python
import jax
import jax.numpy as jnp
from jax import lax

BLOCK = 128
OCC = 128
NT_DEV = 4
NL = 512
NAUX = 1024
NT = 512
N_ORB = 16
N_AUX = 8


def draw_screening(key, part):
    device_count = N_ORB * N_AUX
    sub_keys = jax.random.split(key, device_count + 3)

    def one_order(sub_key):
        return jax.random.permutation(sub_key, NL)[:NT_DEV].astype(jnp.int32)
    orders = jax.vmap(one_order)(sub_keys[:device_count])
    light_count = jax.random.randint(sub_keys[device_count], (device_count,), 1, 3)
    heavy_device = jax.random.randint(sub_keys[device_count + 1], (device_count,), 0, 8) == 0
    forced = jax.random.randint(sub_keys[device_count + 2], (), 0, device_count)
    positions = jnp.arange(device_count, dtype=jnp.int32)
    live_count = jnp.where(heavy_device | (positions == forced), NT_DEV, jnp.minimum(light_count, NT_DEV))
    slot_ids = jnp.arange(NT_DEV, dtype=jnp.int32)
    orbital = jnp.where(slot_ids[None, :] < live_count[:, None], orders, -1)
    window = jnp.broadcast_to((positions // N_AUX)[:, None], orbital.shape)
    auxiliary = jnp.broadcast_to((positions % N_AUX)[:, None], orbital.shape)
    stacked = jnp.stack([window, orbital, auxiliary], axis=-1)
    return stacked.reshape(device_count * NT_DEV, 3).astype(jnp.int32)


def draw_metric_inverse(key, part):
    sampled = jax.random.truncated_normal(key, -4.0, 4.0, (NAUX, NAUX), jnp.float32)
    symmetric = (sampled + sampled.T) * (1.0 / (2.0 * NAUX) ** 0.5)
    return symmetric.astype(jnp.bfloat16)


def block_scale(own_key, extent, cuts, least, high):
    gain = 1.0
    for position, shards_of in cuts:
        steps = jax.random.uniform(jax.random.fold_in(jax.random.fold_in(own_key, 6), position), (shards_of,), jnp.float32, least / len(cuts), high / len(cuts))
        gain = gain * jnp.repeat(jnp.exp(steps), extent[position] // shards_of).reshape((-1,) + (1,) * (len(extent) - 1 - position))
    return gain


def centred(stream_key, shape, spread, limit, cuts=(), held_as=jnp.bfloat16):
    result = jax.random.normal(stream_key, shape, jnp.float32) * spread
    if len(cuts) > 0:
        result = block_scale(stream_key, shape, cuts, -0.22, 0.18) * result
    return jnp.clip(result, min=-limit, max=limit).astype(held_as)


def setup_inputs(seed: int = 0) -> dict:
    arg_keys = jax.random.split(jax.random.key(seed), 5)
    three_center = centred(arg_keys[0], (NT, BLOCK, BLOCK, BLOCK), BLOCK ** -0.5, 0.5, ((0, 128),))
    screening = draw_screening(jax.random.fold_in(arg_keys[4], 71), 0)
    density_factor = centred(arg_keys[2], (NL * BLOCK, OCC), 0.04, 0.23925781, ((0, 16),))
    metric_inverse = draw_metric_inverse(jax.random.fold_in(arg_keys[4], 71), 0)
    return {"three_center": three_center, "screening": screening, "density_factor": density_factor, "metric_inverse": metric_inverse}


def keep_same(current):
    return current


def reference(three_center, screening, density_factor, metric_inverse):
    slot_total = three_center.shape[0]
    factor_blocks = density_factor.reshape(NL, BLOCK, OCC)

    def pair_half(group):
        window_id = group // N_AUX
        aux_id = group % N_AUX

        def one_slot(slot_index, carried):
            orbital = screening[slot_index, 1]
            hit = (screening[slot_index, 0] == window_id) & (screening[slot_index, 2] == aux_id) & (orbital >= 0)

            def add_tile(current):
                row_block = lax.dynamic_index_in_dim(factor_blocks, jnp.maximum(orbital, 0), 0, keepdims=False)
                tile_now = lax.dynamic_index_in_dim(three_center, slot_index, 0, keepdims=False)
                return current + jnp.einsum("mlp,li->mip", tile_now.astype(jnp.float32), row_block.astype(jnp.float32))

            return lax.cond(hit, add_tile, keep_same, carried)

        zero_start = jnp.zeros((BLOCK, OCC, BLOCK), jnp.float32)
        summed = lax.fori_loop(0, slot_total, one_slot, zero_start)
        return summed.astype(jnp.bfloat16)

    halves = lax.map(pair_half, jnp.arange(N_ORB * N_AUX, dtype=jnp.int32))
    halves = halves.reshape(N_ORB, N_AUX, BLOCK, OCC, BLOCK).transpose(0, 2, 3, 1, 4).reshape(N_ORB, BLOCK, OCC, NAUX)
    metric_full = metric_inverse.astype(jnp.float32)

    def window_row(window_id):
        own_half = halves[window_id].astype(jnp.float32)
        next_half = halves[(window_id + 1) % N_ORB].astype(jnp.float32)
        fitted = jnp.einsum("miP,PQ->miQ", own_half, metric_full).astype(jnp.bfloat16)
        fitted = lax.optimization_barrier(fitted).astype(jnp.float32)
        diagonal = jnp.einsum("miq,niq->mn", fitted, own_half)
        coupling = jnp.einsum("miq,niq->mn", fitted, next_half)
        return jnp.concatenate([diagonal, coupling], axis=1).astype(jnp.bfloat16)

    blocks_out = lax.map(window_row, jnp.arange(N_ORB, dtype=jnp.int32))
    return blocks_out.reshape(N_ORB * BLOCK, 2 * BLOCK)
```

```python
import jax
import jax.numpy as jnp
from jax import lax
from jax.experimental import pallas as pl
from jax.experimental.pallas import tpu as pltpu
from jax.sharding import PartitionSpec as P

MESH = pl.DeviceIdType.MESH
B = 128
F32 = jnp.float32
BF16 = jnp.bfloat16


def place():
    orb, aux = lax.axis_index("orb"), lax.axis_index("aux")
    return aux % 4, (aux // 4) * 2 + (orb // 2) % 2, orb // 4, orb % 2


def device(x, y, z, c):
    x, y, z = (x + 4) % 4, (y + 4) % 4, (z + 4) % 4
    return (z * 4 + (y % 2) * 2 + c, (y // 2) * 4 + x)


def lanes(parts):
    return jnp.concatenate(parts, axis=1)


def rows(parts):
    return jnp.concatenate(parts, axis=0)


def kernel(
    t_hbm, scr_ref, d_hbm, j_hbm, o_ref,
    tiles, metric, owned, wants, wants_s, y_out, y_in, z_out, z_in, factor_t, perm,
    half, mid_x, mid_y, own, foll, total, red_in, gathered,
    t_sem, j_sem, d_sem, sib_sem, w_sem, ws_sem, y_sem, z_sem, s1_sem, s2_sem, l1_sem, l2_sem, f_sem, r_sem, g_sem,
):
    x, y, z, c = place()

    load_d = pltpu.make_async_copy(d_hbm, owned.at[pl.ds(c * 32, 32)], d_sem)
    load_d.start()
    load_t = []
    for g in range(8):
        span = pl.ds(g * 16, 16)
        load_t.append(pltpu.make_async_copy(t_hbm.at[:, span], tiles.at[:, span], t_sem.at[g]))
    load_j = pltpu.make_async_copy(j_hbm, metric, j_sem)
    for copy in load_t:
        copy.start()
    load_j.start()

    wants[0, z, pl.ds(0, 4), pl.ds(0, 3)] = scr_ref[...]

    plane = [(dx, dy) for dx in range(4) for dy in range(4) if (dx, dy) != (0, 0)]
    above = [(dy, dz) for dy in (0, 1, 3) for dz in (1, 2, 3)]
    barrier = pltpu.get_barrier_semaphore()
    peers = [device(x, y, z, 1 - c), device(x, y, z + 2 * c - 1, 1 - c)]
    peers += [device(x, y + dy, z + dz, c) for dy, dz in above]
    peers += [device(x + dx, y + dy, z, c) for dx, dy in plane]
    for peer in peers:
        pl.semaphore_signal(barrier, inc=1, device_id=peer, device_id_type=MESH)
    r = lax.broadcasted_iota(jnp.int32, (256, 256), 0)
    k = lax.broadcasted_iota(jnp.int32, (256, 256), 1)
    perm[...] = jnp.where((r % 16) * 16 + r // 16 == k, 1.0, 0.0).astype(BF16)
    pl.semaphore_wait(barrier, len(peers))

    def remote(src, dst, send, recv, peer):
        copy = pltpu.make_async_remote_copy(
            src_ref=src, dst_ref=dst, send_sem=send, recv_sem=recv, device_id=peer, device_id_type=MESH
        )
        copy.start()
        return copy

    sent = []

    want_copies = []
    for n, (dy, dz) in enumerate([(1, 0), (3, 0)] + above):
        slot = {0: 0, 1: 1, 3: 2}[dy]
        want_copies.append(
            remote(wants.at[0, z], wants.at[slot, z], w_sem.at[0, n], w_sem.at[1, n], device(x, y + dy, z + dz, c))
        )
    span = pl.ds(c * 32, 32)
    sibling = remote(d_hbm, owned.at[span], sib_sem.at[0], sib_sem.at[1], device(x, y, z, 1 - c))
    for copy in want_copies:
        copy.wait()
    to_scalar = pltpu.make_async_copy(wants, wants_s, ws_sem)
    to_scalar.start()
    load_d.wait()
    sibling.wait()
    to_scalar.wait()

    first = (z * 4 + (y % 2) * 2) * 32

    def pick(column, zz, slot):
        block = wants_s[column, zz, slot, 1] - first
        inside = (block >= 0) & (block < 64)
        found = owned[jnp.clip(block, 0, 63)]
        return jnp.where(inside, found, jnp.zeros_like(found))

    y_copies = []
    for sub in range(2):
        for way in range(2):
            @pl.loop(0, 4)
            def _(zz):
                y_out[sub, way, zz] = pick(2 - way, zz, way * 2 + sub)

            y_copies.append(
                remote(
                    y_out.at[sub, way], y_in.at[sub, way], y_sem.at[0, sub, way], y_sem.at[1, sub, way],
                    device(x, y + 1 - 2 * way, z, c),
                )
            )
    z_copies = []
    for sub in range(2):
        for way in range(2):
            y_copies[sub * 2 + way].wait()

            @pl.loop(0, 4)
            def _(zz):
                z_out[sub, zz, way] = pick(0, zz, way * 2 + sub) + y_in[sub, way, zz]

        for dz in (2, 1, 3):
            z_copies.append(
                remote(
                    z_out.at[sub, (z + dz) % 4], z_in.at[sub, dz - 1], z_sem.at[0, sub, dz], z_sem.at[1, sub, dz],
                    device(x, y, z + dz, c),
                )
            )
    for copy in z_copies:
        copy.wait()
    for slot in range(4):
        way, sub = slot // 2, slot % 2
        block = z_out[sub, z, way]
        for dz in range(3):
            block = block + z_in[sub, dz, way]
        factor_t[:, pl.ds(slot * B, B)] = block.astype(F32).T.astype(BF16)

    for copy in load_t:
        copy.wait()

    @pl.loop(0, 8)
    def _(g):
        made = []
        for pair in range(8):
            m = g * 16 + pair * 2
            right = rows([lanes([tiles[t, m], tiles[t, m + 1]]) for t in range(4)])
            out = jnp.dot(factor_t[...], right, preferred_element_type=F32).astype(BF16)
            made += [out[:, :B], out[:, B:]]
        for group in range(0, 8, 2):
            stack = lanes([rows([one[(group + e) * 16:(group + e + 1) * 16] for one in made]) for e in range(2)])
            turned = jnp.dot(perm[...], stack, preferred_element_type=F32).astype(BF16)
            for e in range(2):
                for i in range(16):
                    half[(group + e) * 16 + i, pl.ds(pl.multiple_of(g * 16, 16), 16), :] = turned[
                        i * 16:(i + 1) * 16, e * B:(e + 1) * B
                    ]

    def first_hop(chunk):
        n, odd = chunk // 2, chunk % 2
        at = y if odd else x
        land = mid_y.at[n, y // 2, y % 2] if odd else mid_x.at[n, x]
        copies = []
        for d in (2, 1, 3):
            there = (at + d) % 4
            peer = device(x, y + d, z, c) if odd else device(x + d, y, z, c)
            copies.append(
                remote(half.at[pl.ds(chunk * 16 + there * 4, 4)], land, s1_sem.at[0, chunk, d], s1_sem.at[1, chunk, d], peer)
            )
        stays = pltpu.make_async_copy(half.at[pl.ds(chunk * 16 + at * 4, 4)], land, l1_sem.at[chunk])
        stays.start()
        return copies + [stays]

    def second_hop(chunk):
        n, odd = chunk // 2, chunk % 2
        at = x if odd else y
        land = own.at[chunk, :, :, x] if odd else own.at[chunk, y // 2, y % 2]
        copies = []
        for d in (2, 1, 3):
            there = (at + d) % 4
            peer = device(x + d, y, z, c) if odd else device(x, y + d, z, c)
            source = mid_y.at[n, :, :, there] if odd else mid_x.at[n, :, there]
            copies.append(remote(source, land, s2_sem.at[0, chunk, d], s2_sem.at[1, chunk, d], peer))
        source = mid_y.at[n, :, :, at] if odd else mid_x.at[n, :, at]
        stays = pltpu.make_async_copy(source, land, l2_sem.at[chunk])
        stays.start()
        return copies + [stays]

    def follow(chunk):
        a = remote(
            own.at[chunk, :, 1 - c], foll.at[chunk, 0], f_sem.at[0, chunk, 0], f_sem.at[1, chunk, 0], device(x, y, z, 1 - c)
        )
        b = remote(
            own.at[chunk, :, c], foll.at[chunk, 1], f_sem.at[0, chunk, 1], f_sem.at[1, chunk, 1],
            device(x, y, z - (1 - c), 1 - c),
        )
        return [a, b]

    def done(copies):
        for copy in copies:
            copy.wait()

    def own_rows(chunk, s):
        return lanes([own[chunk, h, s, e] for h in range(2) for e in range(4)])

    def foll_rows(chunk, s):
        return lanes([foll[chunk, s, h, e] for h in range(2) for e in range(4)])

    total[...] = jnp.zeros_like(total)

    def finish(pair, hops):
        follows = []
        for e in range(2):
            done(hops[e])
            follows += follow(pair * 2 + e)
        fitted = []
        for e in range(2):
            stack = rows([own_rows(pair * 2 + e, s) for s in range(2)])
            fitted.append(jnp.dot(stack, metric[...], preferred_element_type=F32).astype(BF16))
        done(follows)
        for e in range(2):
            for s in range(2):
                right = rows([own_rows(pair * 2 + e, s), foll_rows(pair * 2 + e, s)])
                total[s] += lax.dot_general(
                    fitted[e][s * B:(s + 1) * B], right, (((1,), (1,)), ((), ())), preferred_element_type=F32
                )

    load_j.wait()
    hop1 = {n: first_hop(n) for n in range(4)}
    hop2 = {}
    for pair in range(4):
        for e in range(2):
            done(hop1[pair * 2 + e])
            hop2[pair * 2 + e] = second_hop(pair * 2 + e)
        if pair < 2:
            for e in range(2):
                hop1[pair * 2 + 4 + e] = first_hop(pair * 2 + 4 + e)
        if pair > 0:
            finish(pair - 1, [hop2[pair * 2 - 2], hop2[pair * 2 - 1]])
    finish(3, [hop2[6], hop2[7]])

    def share(xx, yy):
        return pl.ds(pl.multiple_of((((yy + 4) % 4) // 2 * 4 + (xx + 4) % 4) * 16, 16), 16)

    parts = []
    for n, (dx, dy) in enumerate(plane):
        parts.append(
            remote(
                total.at[(y + dy) % 2, share(x + dx, y + dy)], red_in.at[n], r_sem.at[0, n], r_sem.at[1, n],
                device(x + dx, y + dy, z, c),
            )
        )
    result = total[y % 2, share(x, y), :]
    done(parts)
    for n in range(len(plane)):
        result = result + red_in[n]
    gathered[share(x, y), :] = result.astype(BF16)
    parts = []
    for n, (dx, dy) in enumerate([p for p in plane if p[1] % 2 == 0]):
        parts.append(
            remote(
                gathered.at[share(x, y)], gathered.at[share(x, y)], g_sem.at[0, n], g_sem.at[1, n],
                device(x + dx, y + dy, z, c),
            )
        )
    done(parts)
    o_ref[...] = gathered[...]


def on_device(three_center, screening, density_factor, metric_inverse):
    dma = pltpu.SemaphoreType.DMA
    return pl.pallas_call(
        kernel,
        out_shape=jax.ShapeDtypeStruct((B, 2 * B), BF16),
        in_specs=[
            pl.BlockSpec(memory_space=pl.ANY),
            pl.BlockSpec(memory_space=pltpu.VMEM),
            pl.BlockSpec(memory_space=pl.ANY),
            pl.BlockSpec(memory_space=pl.ANY),
        ],
        out_specs=pl.BlockSpec(memory_space=pltpu.VMEM),
        scratch_shapes=[
            pltpu.VMEM((4, B, B, B), BF16),
            pltpu.VMEM((1024, 1024), BF16),
            pltpu.VMEM((64, B, B), BF16),
            pltpu.VMEM((3, 4, 8, B), jnp.int32),
            pltpu.SMEM((3, 4, 8, B), jnp.int32),
            pltpu.VMEM((2, 2, 4, B, B), BF16),
            pltpu.VMEM((2, 2, 4, B, B), BF16),
            pltpu.VMEM((2, 4, 2, B, B), BF16),
            pltpu.VMEM((2, 3, 2, B, B), BF16),
            pltpu.VMEM((B, 4 * B), BF16),
            pltpu.VMEM((256, 256), BF16),
            pltpu.VMEM((B, B, B), BF16),
            pltpu.VMEM((4, 4, 4, B, B), BF16),
            pltpu.VMEM((4, 2, 2, 4, B, B), BF16),
            pltpu.VMEM((8, 2, 2, 4, B, B), BF16),
            pltpu.VMEM((8, 2, 2, 4, B, B), BF16),
            pltpu.VMEM((2, B, 2 * B), F32),
            pltpu.VMEM((15, 16, 2 * B), F32),
            pltpu.VMEM((B, 2 * B), BF16),
            dma((8,)),
            dma,
            dma,
            dma((2,)),
            dma((2, 11)),
            dma,
            dma((2, 2, 2)),
            dma((2, 2, 4)),
            dma((2, 8, 4)),
            dma((2, 8, 4)),
            dma((8,)),
            dma((8,)),
            dma((2, 8, 2)),
            dma((2, 15)),
            dma((2, 7)),
        ],
        compiler_params=pltpu.CompilerParams(
            collective_id=0, has_side_effects=True, vmem_limit_bytes=56 * 1024 * 1024
        ),
        cost_estimate=pl.CostEstimate(flops=8_000_000_000, bytes_accessed=20_000_000, transcendentals=0),
    )(three_center, screening, density_factor.reshape(-1, B, B), metric_inverse)


def solution(mesh):
    placed = (P(("orb", "aux"), None, None, None), P(("orb", "aux"), None), P("orb", None), P())
    return jax.shard_map(
        on_device, mesh=mesh, in_specs=placed, out_specs=P("orb", None), check_vma=False
    )
```

```python
import jax
import jax.numpy as jnp
from jax import lax
from jax.experimental import pallas as pl
from jax.experimental.pallas import tpu as pltpu
from jax.sharding import PartitionSpec as P

MESH = pl.DeviceIdType.MESH
B = 128
F32 = jnp.float32
BF16 = jnp.bfloat16


def place():
    orb, aux = lax.axis_index("orb"), lax.axis_index("aux")
    return aux % 4, (aux // 4) * 2 + (orb // 2) % 2, orb // 4, orb % 2


def device(x, y, z, c):
    x, y, z = (x + 4) % 4, (y + 4) % 4, (z + 4) % 4
    return (z * 4 + (y % 2) * 2 + c, (y // 2) * 4 + x)


def lanes(parts):
    return jnp.concatenate(parts, axis=1)


def rows(parts):
    return jnp.concatenate(parts, axis=0)


PARTS = ((0, 32), (32, 96))


def kernel(
    t_hbm, scr_ref, d_hbm, j_hbm, o_ref,
    tiles, metric, plain, owned, wants, wants_s, y_out0, y_out1, y_in0, y_in1, z_out0, z_out1, z_in0, z_in1, factor_t, perm,
    half, mid_x, mid_y, own, foll, fitted, diagonal, coupling, red_in, gathered,
    t_sem, j_sem, d_sem, sib_sem, w_sem, ws_sem, y_sem, z_sem, s1_out, s1_in, s2_out, s2_in, f_sem, r_sem, g_sem,
):
    x, y, z, c = place()
    y_out, y_in, z_out, z_in = (y_out0, y_out1), (y_in0, y_in1), (z_out0, z_out1), (z_in0, z_in1)

    load_d = pltpu.make_async_copy(d_hbm, plain, d_sem)
    load_d.start()
    load_t = []
    for g in range(2):
        span = pl.ds(g * 64, 64)
        load_t.append(pltpu.make_async_copy(t_hbm.at[:, span], tiles.at[:, span], t_sem.at[g]))
    load_j = pltpu.make_async_copy(j_hbm, metric, j_sem)
    for copy in load_t:
        copy.start()
    load_j.start()

    wants[0, z, pl.ds(0, 4), pl.ds(0, 3)] = scr_ref[...]

    plane = [(dx, dy) for dx in range(4) for dy in range(4) if (dx, dy) != (0, 0)]
    above = [(dy, dz) for dy in (1, 3, 0) for dz in (0, 1, 2, 3) if (dy, dz) != (0, 0)]
    barrier = pltpu.get_barrier_semaphore()
    peers = [device(x, y, z, 1 - c), device(x, y, z + 2 * c - 1, 1 - c)]
    peers += [device(x, y + dy, z + dz, c) for dy, dz in above if dz]
    peers += [device(x + dx, y + dy, z, c) for dx, dy in plane]
    for peer in peers:
        pl.semaphore_signal(barrier, inc=1, device_id=peer, device_id_type=MESH)

    r = lax.broadcasted_iota(jnp.int32, (256, 256), 0)
    k = lax.broadcasted_iota(jnp.int32, (256, 256), 1)
    perm[...] = jnp.where((r % 16) * 16 + r // 16 == k, 1.0, 0.0).astype(BF16)
    diagonal[...] = jnp.zeros_like(diagonal)
    coupling[...] = jnp.zeros_like(coupling)

    load_d.wait()

    @pl.loop(0, 8)
    def _(n):
        for e in range(4):
            owned[c * 32 + n * 4 + e] = plain[n * 4 + e].T

    pl.semaphore_wait(barrier, len(peers))

    def remote(src, dst, send, recv, peer):
        copy = pltpu.make_async_remote_copy(
            src_ref=src, dst_ref=dst, send_sem=send, recv_sem=recv, device_id=peer, device_id_type=MESH
        )
        copy.start()
        return copy

    def done(sem, ref):
        pltpu.make_async_copy(ref, ref, sem).wait()

    for n, (dy, dz) in enumerate(above):
        slot = {0: 0, 1: 1, 3: 2}[dy]
        group = 0 if dy else 1
        remote(wants.at[0, z], wants.at[slot, z], w_sem.at[0, group], w_sem.at[1, group], device(x, y + dy, z + dz, c))
    span = pl.ds(c * 32, 32)
    sibling = remote(owned.at[span], owned.at[span], sib_sem.at[0], sib_sem.at[1], device(x, y, z, 1 - c))
    others, column = pl.ds(1, 2), pl.ds(0, 3)
    done(w_sem.at[1, 0], wants.at[others])
    others_s = pltpu.make_async_copy(wants.at[others], wants_s.at[others], ws_sem.at[0])
    others_s.start()
    done(w_sem.at[1, 1], wants.at[0, column])
    column_s = pltpu.make_async_copy(wants.at[0], wants_s.at[0], ws_sem.at[1])
    column_s.start()
    sibling.wait_recv()
    others_s.wait()

    first = (z * 4 + (y % 2) * 2) * 32

    def pick(column, zz, slot, part):
        block = wants_s[column, zz, slot, 1] - first
        inside = (block >= 0) & (block < 64)
        start, count = PARTS[part]
        found = owned[jnp.clip(block, 0, 63), pl.ds(start, count), :]
        return jnp.where(inside, found, jnp.zeros_like(found))

    for part in range(2):
        for way in range(2):
            @pl.loop(0, 4)
            def _(zz):
                for sub in range(2):
                    y_out[part][way, zz, sub] = pick(2 - way, zz, way * 2 + sub, part)

            remote(
                y_out[part].at[way], y_in[part].at[way], y_sem.at[0, part], y_sem.at[1, part],
                device(x, y + 1 - 2 * way, z, c),
            )
    column_s.wait()

    def along_z(part):
        done(y_sem.at[1, part], y_in[part])
        for way in range(2):
            @pl.loop(0, 4)
            def _(zz):
                for sub in range(2):
                    z_out[part][zz, way * 2 + sub] = pick(0, zz, way * 2 + sub, part) + y_in[part][way, zz, sub]

        for dz in (2, 1, 3):
            remote(
                z_out[part].at[(z + dz) % 4], z_in[part].at[dz - 1], z_sem.at[0, part], z_sem.at[1, part],
                device(x, y, z + dz, c),
            )

    def arrived(part):
        done(z_sem.at[1, part], z_in[part])
        start, count = PARTS[part]
        for slot in range(4):
            block = z_out[part][z, slot]
            for dz in range(3):
                block = block + z_in[part][dz, slot]
            factor_t[pl.ds(start, count), pl.ds(slot * B, B)] = block

    def transform(part, low, high):
        start, count = PARTS[part]

        @pl.loop(low, high)
        def _(g):
            made = []
            for pair in range(8):
                m = g * 16 + pair * 2
                right = rows([lanes([tiles[t, m], tiles[t, m + 1]]) for t in range(4)])
                out = jnp.dot(
                    factor_t[pl.ds(start, count), :], right, preferred_element_type=F32
                ).astype(BF16)
                made += [out[:, :B], out[:, B:]]
            for group in range(0, count // 16, 2):
                stack = lanes([rows([one[(group + e) * 16:(group + e + 1) * 16] for one in made]) for e in range(2)])
                turned = jnp.dot(perm[...], stack, preferred_element_type=F32).astype(BF16)
                for e in range(2):
                    for i in range(16):
                        half[start + (group + e) * 16 + i, pl.ds(pl.multiple_of(g * 16, 16), 16), :] = turned[
                            i * 16:(i + 1) * 16, e * B:(e + 1) * B
                        ]

    def cut(h):
        return pl.ds(0, B) if h is None else pl.ds(h * 64, 64)

    def first_hop(chunk, h=None):
        n, odd, ms = chunk // 2, chunk % 2, cut(h)
        at = y if odd else x
        land = mid_y.at[n, y // 2, y % 2, :, ms] if odd else mid_x.at[n, x, :, ms]
        for d in (2, 1, 3):
            there = (at + d) % 4
            peer = device(x, y + d, z, c) if odd else device(x + d, y, z, c)
            remote(half.at[pl.ds(chunk * 16 + there * 4, 4), ms], land, s1_out.at[n], s1_in.at[chunk], peer)
        pltpu.make_async_copy(half.at[pl.ds(chunk * 16 + at * 4, 4), ms], land, s1_in.at[chunk]).start()

    def second_hop(chunk, h=None):
        n, odd, ms = chunk // 2, chunk % 2, cut(h)
        into = chunk if h is None else 6 + 2 * h + odd
        at = x if odd else y
        land = own.at[chunk, :, :, x, ms] if odd else own.at[chunk, y // 2, y % 2, :, ms]
        for d in (2, 1, 3):
            there = (at + d) % 4
            peer = device(x + d, y, z, c) if odd else device(x, y + d, z, c)
            source = mid_y.at[n, :, :, there, ms] if odd else mid_x.at[n, :, there, ms]
            remote(source, land, s2_out.at[n], s2_in.at[into], peer)
        source = mid_y.at[n, :, :, at, ms] if odd else mid_x.at[n, :, at, ms]
        pltpu.make_async_copy(source, land, s2_in.at[into]).start()

    def follow(chunk, h=None):
        ms, sem = cut(h), chunk // 2 + (h or 0)
        remote(
            own.at[chunk, :, c, :, ms], foll.at[chunk, 1, :, :, ms], f_sem.at[0, sem], f_sem.at[1, sem],
            device(x, y, z - (1 - c), 1 - c),
        )
        remote(
            own.at[chunk, :, 1 - c, :, ms], foll.at[chunk, 0, :, :, ms], f_sem.at[0, sem], f_sem.at[1, sem],
            device(x, y, z, 1 - c),
        )

    def first_done(pair):
        done(s1_in.at[pair * 2], mid_x.at[pair])
        done(s1_in.at[pair * 2 + 1], mid_y.at[pair])

    def second_done(pair, h=None):
        size = own.at[0, :, :, :, cut(h)]
        for e in range(2):
            done(s2_in.at[pair * 2 + e + 2 * (h or 0)], size)

    def follow_done(pair, h=None):
        done(f_sem.at[1, pair + (h or 0)], foll.at[pl.ds(0, 2), :, :, :, cut(h)])

    def both(hop, pair, h=None):
        for e in range(2):
            hop(pair * 2 + e, h)

    def own_rows(chunk, s):
        return lanes([own[chunk, g, s, e] for g in range(2) for e in range(4)])

    def foll_rows(chunk, s):
        return lanes([foll[chunk, s, g, e] for g in range(2) for e in range(4)])

    def across(left, right):
        return lax.dot_general(left, right, (((1,), (1,)), ((), ())), preferred_element_type=F32)

    def with_itself(pair):
        for e in range(2):
            chunk = pair * 2 + e
            stack = rows([own_rows(chunk, s) for s in range(2)])
            fitted[pair % 2, e] = jnp.dot(stack, metric[...], preferred_element_type=F32).astype(BF16)
            for s in range(2):
                diagonal[s] += across(fitted[pair % 2, e, pl.ds(s * B, B), :], own_rows(chunk, s))

    def with_next(pair):
        for e in range(2):
            for s in range(2):
                coupling[s] += across(fitted[pair % 2, e, pl.ds(s * B, B), :], foll_rows(pair * 2 + e, s))

    along_z(0)
    along_z(1)
    arrived(0)
    load_t[0].wait()
    transform(0, 0, 4)
    both(first_hop, 0, 0)
    load_t[1].wait()
    transform(0, 4, 8)
    both(first_hop, 0, 1)
    arrived(1)
    transform(1, 0, 4)
    both(first_hop, 1, 0)
    transform(1, 4, 6)
    first_done(0)
    both(second_hop, 0)
    transform(1, 6, 8)
    both(first_hop, 1, 1)
    both(first_hop, 2)
    load_j.wait()
    first_done(1)
    both(second_hop, 1)
    both(first_hop, 3)
    second_done(0)
    both(follow, 0)
    with_itself(0)
    first_done(2)
    both(second_hop, 2)
    follow_done(0)
    with_next(0)
    second_done(1)
    both(follow, 1)
    with_itself(1)
    first_done(3)
    both(second_hop, 3, 0)
    both(second_hop, 3, 1)
    follow_done(1)
    with_next(1)
    second_done(2)
    both(follow, 2)
    with_itself(2)
    second_done(3, 0)
    both(follow, 3, 0)
    follow_done(2)
    with_next(2)
    second_done(3, 1)
    both(follow, 3, 1)
    with_itself(3)

    def share(xx, yy):
        return pl.ds(pl.multiple_of((((yy + 4) % 4) // 2 * 4 + (xx + 4) % 4) * 16, 16), 16)

    def scatter(which, summand):
        for n, (dx, dy) in enumerate(plane):
            remote(
                summand.at[(y + dy) % 2, share(x + dx, y + dy)], red_in.at[which, n],
                r_sem.at[0, which], r_sem.at[1, which], device(x + dx, y + dy, z, c),
            )

    def collect(which, summand):
        result = summand[y % 2, share(x, y), :]
        done(r_sem.at[1, which], red_in.at[which])
        for n in range(len(plane)):
            result = result + red_in[which, n]
        gathered[share(x, y), pl.ds(which * B, B)] = result.astype(BF16)

    scatter(0, diagonal)
    follow_done(3, 0)
    follow_done(3, 1)
    with_next(3)
    scatter(1, coupling)
    collect(0, diagonal)
    collect(1, coupling)
    for dx, dy in plane:
        if dy % 2 == 0:
            remote(
                gathered.at[share(x, y)], gathered.at[share(x, y)], g_sem.at[0], g_sem.at[1],
                device(x + dx, y + dy, z, c),
            )

    done(w_sem.at[0, 0], wants.at[others])
    done(w_sem.at[0, 1], wants.at[0, column])
    sibling.wait_send()
    for part in range(2):
        done(y_sem.at[0, part], y_in[part])
        done(z_sem.at[0, part], z_in[part])
    for pair in range(4):
        done(s1_out.at[pair], half.at[pl.ds(0, 24)])
        done(s2_out.at[pair], half.at[pl.ds(0, 24)])
    for pair in range(3):
        done(f_sem.at[0, pair], foll.at[pl.ds(0, 2)])
    for h in range(2):
        done(f_sem.at[0, 3 + h], foll.at[pl.ds(0, 2), :, :, :, cut(h)])
    for which in range(2):
        done(r_sem.at[0, which], red_in.at[which])
    rest = gathered.at[pl.ds(0, 112)]
    done(g_sem.at[0], rest)
    done(g_sem.at[1], rest)
    o_ref[...] = gathered[...]


def on_device(three_center, screening, density_factor, metric_inverse):
    dma = pltpu.SemaphoreType.DMA
    return pl.pallas_call(
        kernel,
        out_shape=jax.ShapeDtypeStruct((B, 2 * B), BF16),
        in_specs=[
            pl.BlockSpec(memory_space=pl.ANY),
            pl.BlockSpec(memory_space=pltpu.VMEM),
            pl.BlockSpec(memory_space=pl.ANY),
            pl.BlockSpec(memory_space=pl.ANY),
        ],
        out_specs=pl.BlockSpec(memory_space=pltpu.VMEM),
        scratch_shapes=[
            pltpu.VMEM((4, B, B, B), BF16),
            pltpu.VMEM((1024, 1024), BF16),
            pltpu.VMEM((32, B, B), BF16),
            pltpu.VMEM((64, B, B), BF16),
            pltpu.VMEM((3, 4, 8, B), jnp.int32),
            pltpu.SMEM((3, 4, 8, B), jnp.int32),
            *[pltpu.VMEM((2, 4, 2, count, B), BF16) for _, count in PARTS],
            *[pltpu.VMEM((2, 4, 2, count, B), BF16) for _, count in PARTS],
            *[pltpu.VMEM((4, 4, count, B), BF16) for _, count in PARTS],
            *[pltpu.VMEM((3, 4, count, B), BF16) for _, count in PARTS],
            pltpu.VMEM((B, 4 * B), BF16),
            pltpu.VMEM((256, 256), BF16),
            pltpu.VMEM((B, B, B), BF16),
            pltpu.VMEM((4, 4, 4, B, B), BF16),
            pltpu.VMEM((4, 2, 2, 4, B, B), BF16),
            pltpu.VMEM((8, 2, 2, 4, B, B), BF16),
            pltpu.VMEM((8, 2, 2, 4, B, B), BF16),
            pltpu.VMEM((2, 2, 2 * B, 1024), BF16),
            pltpu.VMEM((2, B, B), F32),
            pltpu.VMEM((2, B, B), F32),
            pltpu.VMEM((2, 15, 16, B), F32),
            pltpu.VMEM((B, 2 * B), BF16),
            dma((2,)),
            dma,
            dma,
            dma((2,)),
            dma((2, 2)),
            dma((2,)),
            dma((2, 2)),
            dma((2, 2)),
            dma((4,)),
            dma((8,)),
            dma((4,)),
            dma((10,)),
            dma((2, 5)),
            dma((2, 2)),
            dma((2,)),
        ],
        compiler_params=pltpu.CompilerParams(
            collective_id=0, has_side_effects=True, vmem_limit_bytes=44 * 1024 * 1024
        ),
        cost_estimate=pl.CostEstimate(flops=8_000_000_000, bytes_accessed=20_000_000, transcendentals=0),
    )(three_center, screening, density_factor.reshape(-1, B, B), metric_inverse)


def solution(mesh):
    placed = (P(("orb", "aux"), None, None, None), P(("orb", "aux"), None), P("orb", None), P())
    return jax.shard_map(
        on_device, mesh=mesh, in_specs=placed, out_specs=P("orb", None), check_vma=False
    )
```

```python
import jax
import jax.numpy as jnp
from jax import lax
from jax.experimental import pallas as pl
from jax.experimental.pallas import tpu as pltpu
from jax.sharding import PartitionSpec as P

MESH = pl.DeviceIdType.MESH
B = 128
F32 = jnp.float32
BF16 = jnp.bfloat16


def place():
    orb, aux = lax.axis_index("orb"), lax.axis_index("aux")
    return aux % 4, (aux // 4) * 2 + (orb // 2) % 2, orb // 4, orb % 2


def device(x, y, z, c):
    x, y, z = (x + 4) % 4, (y + 4) % 4, (z + 4) % 4
    return (z * 4 + (y % 2) * 2 + c, (y // 2) * 4 + x)


def lanes(parts):
    return jnp.concatenate(parts, axis=1)


def rows(parts):
    return jnp.concatenate(parts, axis=0)


PARTS = ((0, 32), (32, 96))


def kernel(
    t_hbm, scr_ref, d_hbm, j_hbm, o_ref,
    tiles, metric, plain, owned, wants, wants_s, y_out0, y_out1, y_in0, y_in1, z_out0, z_out1, z_in0, z_in1, factor_t, perm,
    half, mid_x, mid_y, own, foll, fitted, diagonal, coupling, red_in, gathered,
    t_sem, j_sem, d_sem, sib_sem, w_sem, ws_sem, y_sem, z_sem, s1_out, s1_in, s2_out, s2_in, f_sem, r_sem, g_sem,
):
    x, y, z, c = place()
    y_out, y_in, z_out, z_in = (y_out0, y_out1), (y_in0, y_in1), (z_out0, z_out1), (z_in0, z_in1)

    load_d = pltpu.make_async_copy(d_hbm, plain, d_sem)
    load_d.start()
    load_t = []
    for g in range(2):
        span = pl.ds(g * 64, 64)
        load_t.append(pltpu.make_async_copy(t_hbm.at[:, span], tiles.at[:, span], t_sem.at[g]))
    load_j = pltpu.make_async_copy(j_hbm, metric, j_sem)

    wants[0, z, pl.ds(0, 4), pl.ds(0, 3)] = scr_ref[...]

    plane = [(dx, dy) for dx in range(4) for dy in range(4) if (dx, dy) != (0, 0)]
    above = [(dy, dz) for dy in (1, 3, 0) for dz in (0, 1, 2, 3) if (dy, dz) != (0, 0)]
    barrier = pltpu.get_barrier_semaphore()
    peers = [device(x, y, z, 1 - c), device(x, y, z + 2 * c - 1, 1 - c)]
    peers += [device(x, y + dy, z + dz, c) for dy, dz in above if dz]
    peers += [device(x + dx, y + dy, z, c) for dx, dy in plane]
    for peer in peers:
        pl.semaphore_signal(barrier, inc=1, device_id=peer, device_id_type=MESH)

    r = lax.broadcasted_iota(jnp.int32, (256, 256), 0)
    k = lax.broadcasted_iota(jnp.int32, (256, 256), 1)
    perm[...] = jnp.where((r % 16) * 16 + r // 16 == k, 1.0, 0.0).astype(BF16)
    diagonal[...] = jnp.zeros_like(diagonal)
    coupling[...] = jnp.zeros_like(coupling)

    load_d.wait()
    load_t[0].start()

    @pl.loop(0, 8)
    def _(n):
        for e in range(4):
            owned[c * 32 + n * 4 + e] = plain[n * 4 + e].T

    pl.semaphore_wait(barrier, len(peers))

    def remote(src, dst, send, recv, peer):
        copy = pltpu.make_async_remote_copy(
            src_ref=src, dst_ref=dst, send_sem=send, recv_sem=recv, device_id=peer, device_id_type=MESH
        )
        copy.start()
        return copy

    def done(sem, ref):
        pltpu.make_async_copy(ref, ref, sem).wait()

    for n, (dy, dz) in enumerate(above):
        slot = {0: 0, 1: 1, 3: 2}[dy]
        group = 0 if dy else 1
        remote(wants.at[0, z], wants.at[slot, z], w_sem.at[0, group], w_sem.at[1, group], device(x, y + dy, z + dz, c))
    span = pl.ds(c * 32, 32)
    sibling = remote(owned.at[span], owned.at[span], sib_sem.at[0], sib_sem.at[1], device(x, y, z, 1 - c))
    others, column = pl.ds(1, 2), pl.ds(0, 3)
    done(w_sem.at[1, 0], wants.at[others])
    others_s = pltpu.make_async_copy(wants.at[others], wants_s.at[others], ws_sem.at[0])
    others_s.start()
    done(w_sem.at[1, 1], wants.at[0, column])
    column_s = pltpu.make_async_copy(wants.at[0], wants_s.at[0], ws_sem.at[1])
    column_s.start()
    sibling.wait_recv()
    others_s.wait()

    first = (z * 4 + (y % 2) * 2) * 32

    def pick(column, zz, slot, part):
        block = wants_s[column, zz, slot, 1] - first
        inside = (block >= 0) & (block < 64)
        start, count = PARTS[part]
        found = owned[jnp.clip(block, 0, 63), pl.ds(start, count), :]
        return jnp.where(inside, found, jnp.zeros_like(found))

    for part in range(2):
        for way in range(2):
            @pl.loop(0, 4, unroll=True)
            def _(zz):
                for sub in range(2):
                    y_out[part][way, zz, sub] = pick(2 - way, zz, way * 2 + sub, part)

            remote(
                y_out[part].at[way], y_in[part].at[way], y_sem.at[0, part], y_sem.at[1, part],
                device(x, y + 1 - 2 * way, z, c),
            )
    column_s.wait()
    load_t[1].start()
    load_j.start()

    def along_z(part):
        done(y_sem.at[1, part], y_in[part])
        for way in range(2):
            @pl.loop(0, 4, unroll=True)
            def _(zz):
                for sub in range(2):
                    z_out[part][zz, way * 2 + sub] = pick(0, zz, way * 2 + sub, part) + y_in[part][way, zz, sub]

        for dz in (2, 1, 3):
            remote(
                z_out[part].at[(z + dz) % 4], z_in[part].at[dz - 1], z_sem.at[0, part], z_sem.at[1, part],
                device(x, y, z + dz, c),
            )

    def arrived(part):
        done(z_sem.at[1, part], z_in[part])
        start, count = PARTS[part]
        for slot in range(4):
            block = z_out[part][z, slot]
            for dz in range(3):
                block = block + z_in[part][dz, slot]
            factor_t[pl.ds(start, count), pl.ds(slot * B, B)] = block

    def transform(part, low, high):
        start, count = PARTS[part]

        @pl.loop(low, high)
        def _(g):
            made = []
            for pair in range(8):
                m = g * 16 + pair * 2
                right = rows([lanes([tiles[t, m], tiles[t, m + 1]]) for t in range(4)])
                out = jnp.dot(
                    factor_t[pl.ds(start, count), :], right, preferred_element_type=F32
                ).astype(BF16)
                made += [out[:, :B], out[:, B:]]
            for group in range(0, count // 16, 2):
                stack = lanes([rows([one[(group + e) * 16:(group + e + 1) * 16] for one in made]) for e in range(2)])
                turned = jnp.dot(perm[...], stack, preferred_element_type=F32).astype(BF16)
                for e in range(2):
                    for i in range(16):
                        half[start + (group + e) * 16 + i, pl.ds(pl.multiple_of(g * 16, 16), 16), :] = turned[
                            i * 16:(i + 1) * 16, e * B:(e + 1) * B
                        ]

    def cut(h):
        return pl.ds(0, B) if h is None else pl.ds(h * 64, 64)

    def first_hop(chunk, d, h=None):
        n, odd, ms = chunk // 2, chunk % 2, cut(h)
        at = y if odd else x
        land = mid_y.at[n, y // 2, y % 2, :, ms] if odd else mid_x.at[n, x, :, ms]
        source = half.at[pl.ds(chunk * 16 + (at + d) % 4 * 4, 4), ms]
        if d:
            peer = device(x, y + d, z, c) if odd else device(x + d, y, z, c)
            remote(source, land, s1_out.at[n], s1_in.at[chunk], peer)
        else:
            pltpu.make_async_copy(source, land, s1_in.at[chunk]).start()

    def second_hop(chunk, d, h=None):
        n, odd, ms = chunk // 2, chunk % 2, cut(h)
        into = chunk if h is None else 6 + 2 * h + odd
        there = ((x if odd else y) + d) % 4
        land = own.at[chunk, :, :, x, ms] if odd else own.at[chunk, y // 2, y % 2, :, ms]
        source = mid_y.at[n, :, :, there, ms] if odd else mid_x.at[n, :, there, ms]
        if d:
            peer = device(x + d, y, z, c) if odd else device(x, y + d, z, c)
            remote(source, land, s2_out.at[n], s2_in.at[into], peer)
        else:
            pltpu.make_async_copy(source, land, s2_in.at[into]).start()

    def follow(chunk, h=None):
        ms, sem = cut(h), chunk // 2 + (h or 0)
        remote(
            own.at[chunk, :, c, :, ms], foll.at[chunk, 1, :, :, ms], f_sem.at[0, sem], f_sem.at[1, sem],
            device(x, y, z - (1 - c), 1 - c),
        )
        remote(
            own.at[chunk, :, 1 - c, :, ms], foll.at[chunk, 0, :, :, ms], f_sem.at[0, sem], f_sem.at[1, sem],
            device(x, y, z, 1 - c),
        )

    def first_done(pair):
        done(s1_in.at[pair * 2], mid_x.at[pair])
        done(s1_in.at[pair * 2 + 1], mid_y.at[pair])

    def second_done(pair, h=None):
        size = own.at[0, :, :, :, cut(h)]
        for e in range(2):
            done(s2_in.at[pair * 2 + e + 2 * (h or 0)], size)

    def follow_done(pair, h=None):
        done(f_sem.at[1, pair + (h or 0)], foll.at[pl.ds(0, 2), :, :, :, cut(h)])

    def both(hop, pair, h=None):
        for d in (1, 3, 2, 0):
            for e in range(2):
                hop(pair * 2 + e, d, h)

    def follow_both(pair, h=None):
        for e in range(2):
            follow(pair * 2 + e, h)

    def own_rows(chunk, s):
        return lanes([own[chunk, g, s, e] for g in range(2) for e in range(4)])

    def foll_rows(chunk, s):
        return lanes([foll[chunk, s, g, e] for g in range(2) for e in range(4)])

    def across(left, right):
        return lax.dot_general(left, right, (((1,), (1,)), ((), ())), preferred_element_type=F32)

    def with_itself(pair):
        for e in range(2):
            chunk = pair * 2 + e
            stack = rows([own_rows(chunk, s) for s in range(2)])
            fitted[pair % 2, e] = jnp.dot(stack, metric[...], preferred_element_type=F32).astype(BF16)
            for s in range(2):
                diagonal[s] += across(fitted[pair % 2, e, pl.ds(s * B, B), :], own_rows(chunk, s))

    def with_next(pair):
        for e in range(2):
            for s in range(2):
                coupling[s] += across(fitted[pair % 2, e, pl.ds(s * B, B), :], foll_rows(pair * 2 + e, s))

    along_z(0)
    arrived(0)
    load_t[0].wait()
    transform(0, 0, 2)
    along_z(1)
    transform(0, 2, 4)
    both(first_hop, 0, 0)
    load_t[1].wait()
    transform(0, 4, 8)
    both(first_hop, 0, 1)
    arrived(1)
    transform(1, 0, 4)
    both(first_hop, 1, 0)
    first_done(0)
    both(second_hop, 0)
    transform(1, 4, 8)
    both(first_hop, 1, 1)
    both(first_hop, 2)
    load_j.wait()
    first_done(1)
    both(second_hop, 1)
    both(first_hop, 3)
    second_done(0)
    follow_both(0)
    with_itself(0)
    first_done(2)
    both(second_hop, 2)
    follow_done(0)
    with_next(0)
    second_done(1)
    follow_both(1)
    with_itself(1)
    first_done(3)
    both(second_hop, 3, 0)
    both(second_hop, 3, 1)
    follow_done(1)
    with_next(1)
    second_done(2)
    follow_both(2)
    with_itself(2)
    second_done(3, 0)
    follow_both(3, 0)
    follow_done(2)
    with_next(2)
    second_done(3, 1)
    follow_both(3, 1)
    with_itself(3)

    def share(xx, yy):
        return pl.ds(pl.multiple_of((((yy + 4) % 4) // 2 * 4 + (xx + 4) % 4) * 16, 16), 16)

    def scatter(which, summand):
        for n, (dx, dy) in enumerate(plane):
            remote(
                summand.at[(y + dy) % 2, share(x + dx, y + dy)], red_in.at[which, n],
                r_sem.at[0, which], r_sem.at[1, which], device(x + dx, y + dy, z, c),
            )

    def collect(which, summand):
        result = summand[y % 2, share(x, y), :]
        done(r_sem.at[1, which], red_in.at[which])
        for n in range(len(plane)):
            result = result + red_in[which, n]
        gathered[share(x, y), pl.ds(which * B, B)] = result.astype(BF16)

    scatter(0, diagonal)
    follow_done(3, 0)
    follow_done(3, 1)
    with_next(3)
    scatter(1, coupling)
    collect(0, diagonal)
    collect(1, coupling)
    for dx, dy in plane:
        if dy % 2 == 0:
            remote(
                gathered.at[share(x, y)], gathered.at[share(x, y)], g_sem.at[0], g_sem.at[1],
                device(x + dx, y + dy, z, c),
            )

    done(w_sem.at[0, 0], wants.at[others])
    done(w_sem.at[0, 1], wants.at[0, column])
    sibling.wait_send()
    for part in range(2):
        done(y_sem.at[0, part], y_in[part])
        done(z_sem.at[0, part], z_in[part])
    for pair in range(4):
        done(s1_out.at[pair], half.at[pl.ds(0, 24)])
        done(s2_out.at[pair], half.at[pl.ds(0, 24)])
    for pair in range(3):
        done(f_sem.at[0, pair], foll.at[pl.ds(0, 2)])
    for h in range(2):
        done(f_sem.at[0, 3 + h], foll.at[pl.ds(0, 2), :, :, :, cut(h)])
    for which in range(2):
        done(r_sem.at[0, which], red_in.at[which])
    rest = gathered.at[pl.ds(0, 112)]
    done(g_sem.at[0], rest)
    done(g_sem.at[1], rest)
    o_ref[...] = gathered[...]


def on_device(three_center, screening, density_factor, metric_inverse):
    dma = pltpu.SemaphoreType.DMA
    return pl.pallas_call(
        kernel,
        out_shape=jax.ShapeDtypeStruct((B, 2 * B), BF16),
        in_specs=[
            pl.BlockSpec(memory_space=pl.ANY),
            pl.BlockSpec(memory_space=pltpu.VMEM),
            pl.BlockSpec(memory_space=pl.ANY),
            pl.BlockSpec(memory_space=pl.ANY),
        ],
        out_specs=pl.BlockSpec(memory_space=pltpu.VMEM),
        scratch_shapes=[
            pltpu.VMEM((4, B, B, B), BF16),
            pltpu.VMEM((1024, 1024), BF16),
            pltpu.VMEM((32, B, B), BF16),
            pltpu.VMEM((64, B, B), BF16),
            pltpu.VMEM((3, 4, 8, B), jnp.int32),
            pltpu.SMEM((3, 4, 8, B), jnp.int32),
            *[pltpu.VMEM((2, 4, 2, count, B), BF16) for _, count in PARTS],
            *[pltpu.VMEM((2, 4, 2, count, B), BF16) for _, count in PARTS],
            *[pltpu.VMEM((4, 4, count, B), BF16) for _, count in PARTS],
            *[pltpu.VMEM((3, 4, count, B), BF16) for _, count in PARTS],
            pltpu.VMEM((B, 4 * B), BF16),
            pltpu.VMEM((256, 256), BF16),
            pltpu.VMEM((B, B, B), BF16),
            pltpu.VMEM((4, 4, 4, B, B), BF16),
            pltpu.VMEM((4, 2, 2, 4, B, B), BF16),
            pltpu.VMEM((8, 2, 2, 4, B, B), BF16),
            pltpu.VMEM((8, 2, 2, 4, B, B), BF16),
            pltpu.VMEM((2, 2, 2 * B, 1024), BF16),
            pltpu.VMEM((2, B, B), F32),
            pltpu.VMEM((2, B, B), F32),
            pltpu.VMEM((2, 15, 16, B), F32),
            pltpu.VMEM((B, 2 * B), BF16),
            dma((2,)),
            dma,
            dma,
            dma((2,)),
            dma((2, 2)),
            dma((2,)),
            dma((2, 2)),
            dma((2, 2)),
            dma((4,)),
            dma((8,)),
            dma((4,)),
            dma((10,)),
            dma((2, 5)),
            dma((2, 2)),
            dma((2,)),
        ],
        compiler_params=pltpu.CompilerParams(
            collective_id=0, has_side_effects=True, vmem_limit_bytes=54 * 1024 * 1024
        ),
        cost_estimate=pl.CostEstimate(flops=8_000_000_000, bytes_accessed=20_000_000, transcendentals=0),
    )(three_center, screening, density_factor.reshape(-1, B, B), metric_inverse)


def solution(mesh):
    placed = (P(("orb", "aux"), None, None, None), P(("orb", "aux"), None), P("orb", None), P())
    return jax.shard_map(
        on_device, mesh=mesh, in_specs=placed, out_specs=P("orb", None), check_vma=False
    )
```

```python
import jax
import jax.numpy as jnp
from jax import lax
from jax.experimental import pallas as pl
from jax.experimental.pallas import tpu as pltpu
from jax.sharding import PartitionSpec as P

MESH = pl.DeviceIdType.MESH
B = 128
F32 = jnp.float32
BF16 = jnp.bfloat16


def place():
    orb, aux = lax.axis_index("orb"), lax.axis_index("aux")
    return aux % 4, (aux // 4) * 2 + (orb // 2) % 2, orb // 4, orb % 2


def device(x, y, z, c):
    x, y, z = (x + 4) % 4, (y + 4) % 4, (z + 4) % 4
    return (z * 4 + (y % 2) * 2 + c, (y // 2) * 4 + x)


def lanes(parts):
    return jnp.concatenate(parts, axis=1)


def rows(parts):
    return jnp.concatenate(parts, axis=0)


PARTS = ((0, 32), (32, 32), (64, 64))


def kernel(
    t_hbm, scr_ref, d_hbm, j_hbm, o_ref,
    tiles, metric, plain, owned, wants, wants_s, y_out0, y_out1, y_out2, y_in0, y_in1, y_in2,
    z_out0, z_out1, z_out2, z_in0, z_in1, z_in2, factor_t, perm,
    half, mid_x, mid_y, own, foll, fitted, diagonal, coupling, red_in, gathered,
    t_sem, j_sem, d_sem, sib_sem, w_sem, ws_sem, y_sem, z_sem, s1_out, s1_in, s2_out, s2_in, f_sem, r_sem, g_sem,
):
    x, y, z, c = place()
    y_out, y_in = (y_out0, y_out1, y_out2), (y_in0, y_in1, y_in2)
    z_out, z_in = (z_out0, z_out1, z_out2), (z_in0, z_in1, z_in2)

    load_d = pltpu.make_async_copy(d_hbm, plain, d_sem)
    load_d.start()
    load_t = []
    for g in range(2):
        span = pl.ds(g * 64, 64)
        load_t.append(pltpu.make_async_copy(t_hbm.at[:, span], tiles.at[:, span], t_sem.at[g]))
    load_j = pltpu.make_async_copy(j_hbm, metric, j_sem)

    wants[0, z, pl.ds(0, 4), pl.ds(0, 3)] = scr_ref[...]

    plane = [(dx, dy) for dx in range(4) for dy in range(4) if (dx, dy) != (0, 0)]
    above = [(dy, dz) for dy in (1, 3, 0) for dz in (0, 1, 2, 3) if (dy, dz) != (0, 0)]
    barrier = pltpu.get_barrier_semaphore()
    peers = [device(x, y, z, 1 - c), device(x, y, z + 2 * c - 1, 1 - c)]
    peers += [device(x, y + dy, z + dz, c) for dy, dz in above if dz]
    peers += [device(x + dx, y + dy, z, c) for dx, dy in plane]
    for peer in peers:
        pl.semaphore_signal(barrier, inc=1, device_id=peer, device_id_type=MESH)

    r = lax.broadcasted_iota(jnp.int32, (256, 256), 0)
    k = lax.broadcasted_iota(jnp.int32, (256, 256), 1)
    perm[...] = jnp.where((r % 16) * 16 + r // 16 == k, 1.0, 0.0).astype(BF16)
    diagonal[...] = jnp.zeros_like(diagonal)
    coupling[...] = jnp.zeros_like(coupling)

    load_d.wait()
    load_t[0].start()

    @pl.loop(0, 8)
    def _(n):
        for e in range(4):
            owned[c * 32 + n * 4 + e] = plain[n * 4 + e].T

    pl.semaphore_wait(barrier, len(peers))

    def remote(src, dst, send, recv, peer):
        copy = pltpu.make_async_remote_copy(
            src_ref=src, dst_ref=dst, send_sem=send, recv_sem=recv, device_id=peer, device_id_type=MESH
        )
        copy.start()
        return copy

    def done(sem, ref):
        pltpu.make_async_copy(ref, ref, sem).wait()

    for n, (dy, dz) in enumerate(above):
        slot = {0: 0, 1: 1, 3: 2}[dy]
        group = 0 if dy else 1
        remote(wants.at[0, z], wants.at[slot, z], w_sem.at[0, group], w_sem.at[1, group], device(x, y + dy, z + dz, c))
    span = pl.ds(c * 32, 32)
    sibling = remote(owned.at[span], owned.at[span], sib_sem.at[0], sib_sem.at[1], device(x, y, z, 1 - c))
    others, column = pl.ds(1, 2), pl.ds(0, 3)
    done(w_sem.at[1, 0], wants.at[others])
    others_s = pltpu.make_async_copy(wants.at[others], wants_s.at[others], ws_sem.at[0])
    others_s.start()
    done(w_sem.at[1, 1], wants.at[0, column])
    column_s = pltpu.make_async_copy(wants.at[0], wants_s.at[0], ws_sem.at[1])
    column_s.start()
    sibling.wait_recv()
    others_s.wait()

    first = (z * 4 + (y % 2) * 2) * 32

    def pick(column, zz, slot, part):
        block = wants_s[column, zz, slot, 1] - first
        inside = (block >= 0) & (block < 64)
        start, count = PARTS[part]
        found = owned[jnp.clip(block, 0, 63), pl.ds(start, count), :]
        return jnp.where(inside, found, jnp.zeros_like(found))

    for part in range(3):
        for way in range(2):
            @pl.loop(0, 4, unroll=True)
            def _(zz):
                for sub in range(2):
                    y_out[part][way, zz, sub] = pick(2 - way, zz, way * 2 + sub, part)

            remote(
                y_out[part].at[way], y_in[part].at[way], y_sem.at[0, part], y_sem.at[1, part],
                device(x, y + 1 - 2 * way, z, c),
            )
    column_s.wait()
    load_t[1].start()
    load_j.start()

    def along_z(part):
        done(y_sem.at[1, part], y_in[part])
        for way in range(2):
            @pl.loop(0, 4, unroll=True)
            def _(zz):
                for sub in range(2):
                    z_out[part][zz, way * 2 + sub] = pick(0, zz, way * 2 + sub, part) + y_in[part][way, zz, sub]

        for dz in (2, 1, 3):
            remote(
                z_out[part].at[(z + dz) % 4], z_in[part].at[dz - 1], z_sem.at[0, part], z_sem.at[1, part],
                device(x, y, z + dz, c),
            )

    def arrived(part):
        done(z_sem.at[1, part], z_in[part])
        start, count = PARTS[part]
        for slot in range(4):
            block = z_out[part][z, slot]
            for dz in range(3):
                block = block + z_in[part][dz, slot]
            factor_t[pl.ds(start, count), pl.ds(slot * B, B)] = block

    def transform(part, low, high):
        start, count = PARTS[part]

        @pl.loop(low, high)
        def _(g):
            made = []
            for pair in range(8):
                m = g * 16 + pair * 2
                right = rows([lanes([tiles[t, m], tiles[t, m + 1]]) for t in range(4)])
                out = jnp.dot(
                    factor_t[pl.ds(start, count), :], right, preferred_element_type=F32
                ).astype(BF16)
                made += [out[:, :B], out[:, B:]]
            for group in range(0, count // 16, 2):
                stack = lanes([rows([one[(group + e) * 16:(group + e + 1) * 16] for one in made]) for e in range(2)])
                turned = jnp.dot(perm[...], stack, preferred_element_type=F32).astype(BF16)
                for e in range(2):
                    for i in range(16):
                        half[start + (group + e) * 16 + i, pl.ds(pl.multiple_of(g * 16, 16), 16), :] = turned[
                            i * 16:(i + 1) * 16, e * B:(e + 1) * B
                        ]

    def cut(h):
        return {None: pl.ds(0, B), 0: pl.ds(0, 64), 1: pl.ds(64, 64), 2: pl.ds(0, 32), 3: pl.ds(32, 32), 4: pl.ds(64, 32), 5: pl.ds(96, 32)}[h]

    def piece(h):
        return {None: 0, 0: 0, 4: 1, 5: 2}[h]

    def first_hop(chunk, d, h=None):
        n, odd, ms = chunk // 2, chunk % 2, cut(h)
        at = y if odd else x
        land = mid_y.at[n, y // 2, y % 2, :, ms] if odd else mid_x.at[n, x, :, ms]
        source = half.at[pl.ds(chunk * 16 + (at + d) % 4 * 4, 4), ms]
        if d:
            peer = device(x, y + d, z, c) if odd else device(x + d, y, z, c)
            remote(source, land, s1_out.at[n], s1_in.at[chunk], peer)
        else:
            pltpu.make_async_copy(source, land, s1_in.at[chunk]).start()

    def second_hop(chunk, d, h=None):
        n, odd, ms = chunk // 2, chunk % 2, cut(h)
        into = chunk + 2 * piece(h)
        there = ((x if odd else y) + d) % 4
        land = own.at[chunk, :, :, x, ms] if odd else own.at[chunk, y // 2, y % 2, :, ms]
        source = mid_y.at[n, :, :, there, ms] if odd else mid_x.at[n, :, there, ms]
        if d:
            peer = device(x + d, y, z, c) if odd else device(x, y + d, z, c)
            remote(source, land, s2_out.at[n], s2_in.at[into], peer)
        else:
            pltpu.make_async_copy(source, land, s2_in.at[into]).start()

    def follow(chunk, h=None):
        ms, sem = cut(h), chunk // 2 + piece(h)
        remote(
            own.at[chunk, :, c, :, ms], foll.at[chunk, 1, :, :, ms], f_sem.at[0, sem], f_sem.at[1, sem],
            device(x, y, z - (1 - c), 1 - c),
        )
        remote(
            own.at[chunk, :, 1 - c, :, ms], foll.at[chunk, 0, :, :, ms], f_sem.at[0, sem], f_sem.at[1, sem],
            device(x, y, z, 1 - c),
        )

    def first_done(pair):
        done(s1_in.at[pair * 2], mid_x.at[pair])
        done(s1_in.at[pair * 2 + 1], mid_y.at[pair])

    def second_done(pair, h=None):
        size = own.at[0, :, :, :, cut(h)]
        for e in range(2):
            done(s2_in.at[pair * 2 + e + 2 * piece(h)], size)

    def follow_done(pair, h=None):
        done(f_sem.at[1, pair + piece(h)], foll.at[pl.ds(0, 2), :, :, :, cut(h)])

    def both(hop, pair, h=None):
        for d in (1, 3, 2, 0):
            for e in range(2):
                hop(pair * 2 + e, d, h)

    def follow_both(pair, h=None):
        for e in range(2):
            follow(pair * 2 + e, h)

    def own_rows(chunk, s):
        return lanes([own[chunk, g, s, e] for g in range(2) for e in range(4)])

    def foll_rows(chunk, s):
        return lanes([foll[chunk, s, g, e] for g in range(2) for e in range(4)])

    def across(left, right):
        return lax.dot_general(left, right, (((1,), (1,)), ((), ())), preferred_element_type=F32)

    def with_itself(pair):
        for e in range(2):
            chunk = pair * 2 + e
            stack = rows([own_rows(chunk, s) for s in range(2)])
            fitted[pair % 2, e] = jnp.dot(stack, metric[...], preferred_element_type=F32).astype(BF16)
            for s in range(2):
                diagonal[s] += across(fitted[pair % 2, e, pl.ds(s * B, B), :], own_rows(chunk, s))

    def with_next(pair):
        for e in range(2):
            for s in range(2):
                coupling[s] += across(fitted[pair % 2, e, pl.ds(s * B, B), :], foll_rows(pair * 2 + e, s))

    along_z(0)
    along_z(1)
    arrived(0)
    load_t[0].wait()
    transform(0, 0, 2)
    both(first_hop, 0, 2)
    along_z(2)
    transform(0, 2, 4)
    both(first_hop, 0, 3)
    load_t[1].wait()
    transform(0, 4, 8)
    both(first_hop, 0, 1)
    arrived(1)
    transform(1, 0, 4)
    both(first_hop, 1, 0)
    transform(1, 4, 6)
    first_done(0)
    both(second_hop, 0)
    transform(1, 6, 8)
    both(first_hop, 1, 1)
    arrived(2)
    transform(2, 0, 4)
    both(first_hop, 2, 0)
    first_done(1)
    both(second_hop, 1)
    transform(2, 4, 8)
    both(first_hop, 2, 1)
    both(first_hop, 3)
    load_j.wait()
    second_done(0)
    follow_both(0)
    first_done(2)
    both(second_hop, 2)
    with_itself(0)
    second_done(1)
    follow_both(1)
    first_done(3)
    for h in (0, 4, 5):
        both(second_hop, 3, h)
    with_itself(1)
    follow_done(0)
    with_next(0)
    follow_done(1)
    with_next(1)
    second_done(2)
    follow_both(2)
    with_itself(2)
    second_done(3, 0)
    follow_both(3, 0)
    follow_done(2)
    with_next(2)
    for h in (4, 5):
        second_done(3, h)
        follow_both(3, h)
    with_itself(3)

    def share(xx, yy):
        return pl.ds(pl.multiple_of((((yy + 4) % 4) // 2 * 4 + (xx + 4) % 4) * 16, 16), 16)

    def scatter(which, summand):
        for n, (dx, dy) in enumerate(plane):
            remote(
                summand.at[(y + dy) % 2, share(x + dx, y + dy)], red_in.at[which, n],
                r_sem.at[0, which], r_sem.at[1, which], device(x + dx, y + dy, z, c),
            )

    def collect(which, summand):
        result = summand[y % 2, share(x, y), :]
        done(r_sem.at[1, which], red_in.at[which])
        for n in range(len(plane)):
            result = result + red_in[which, n]
        gathered[share(x, y), pl.ds(which * B, B)] = result.astype(BF16)

    scatter(0, diagonal)
    for h in (0, 4, 5):
        follow_done(3, h)
    with_next(3)
    scatter(1, coupling)
    collect(0, diagonal)
    collect(1, coupling)
    for dx, dy in plane:
        if dy % 2 == 0:
            remote(
                gathered.at[share(x, y)], gathered.at[share(x, y)], g_sem.at[0], g_sem.at[1],
                device(x + dx, y + dy, z, c),
            )

    done(w_sem.at[0, 0], wants.at[others])
    done(w_sem.at[0, 1], wants.at[0, column])
    sibling.wait_send()
    for part in range(3):
        done(y_sem.at[0, part], y_in[part])
        done(z_sem.at[0, part], z_in[part])
    for pair in range(4):
        done(s1_out.at[pair], half.at[pl.ds(0, 24)])
        done(s2_out.at[pair], half.at[pl.ds(0, 24)])
    for pair in range(3):
        done(f_sem.at[0, pair], foll.at[pl.ds(0, 2)])
    for h in (0, 4, 5):
        done(f_sem.at[0, 3 + piece(h)], foll.at[pl.ds(0, 2), :, :, :, cut(h)])
    for which in range(2):
        done(r_sem.at[0, which], red_in.at[which])
    rest = gathered.at[pl.ds(0, 112)]
    done(g_sem.at[0], rest)
    done(g_sem.at[1], rest)
    o_ref[...] = gathered[...]


def on_device(three_center, screening, density_factor, metric_inverse):
    dma = pltpu.SemaphoreType.DMA
    return pl.pallas_call(
        kernel,
        out_shape=jax.ShapeDtypeStruct((B, 2 * B), BF16),
        in_specs=[
            pl.BlockSpec(memory_space=pl.ANY),
            pl.BlockSpec(memory_space=pltpu.VMEM),
            pl.BlockSpec(memory_space=pl.ANY),
            pl.BlockSpec(memory_space=pl.ANY),
        ],
        out_specs=pl.BlockSpec(memory_space=pltpu.VMEM),
        scratch_shapes=[
            pltpu.VMEM((4, B, B, B), BF16),
            pltpu.VMEM((1024, 1024), BF16),
            pltpu.VMEM((32, B, B), BF16),
            pltpu.VMEM((64, B, B), BF16),
            pltpu.VMEM((3, 4, 8, B), jnp.int32),
            pltpu.SMEM((3, 4, 8, B), jnp.int32),
            *[pltpu.VMEM((2, 4, 2, count, B), BF16) for _, count in PARTS],
            *[pltpu.VMEM((2, 4, 2, count, B), BF16) for _, count in PARTS],
            *[pltpu.VMEM((4, 4, count, B), BF16) for _, count in PARTS],
            *[pltpu.VMEM((3, 4, count, B), BF16) for _, count in PARTS],
            pltpu.VMEM((B, 4 * B), BF16),
            pltpu.VMEM((256, 256), BF16),
            pltpu.VMEM((B, B, B), BF16),
            pltpu.VMEM((4, 4, 4, B, B), BF16),
            pltpu.VMEM((4, 2, 2, 4, B, B), BF16),
            pltpu.VMEM((8, 2, 2, 4, B, B), BF16),
            pltpu.VMEM((8, 2, 2, 4, B, B), BF16),
            pltpu.VMEM((2, 2, 2 * B, 1024), BF16),
            pltpu.VMEM((2, B, B), F32),
            pltpu.VMEM((2, B, B), F32),
            pltpu.VMEM((2, 15, 16, B), F32),
            pltpu.VMEM((B, 2 * B), BF16),
            dma((2,)),
            dma,
            dma,
            dma((2,)),
            dma((2, 2)),
            dma((2,)),
            dma((2, 3)),
            dma((2, 3)),
            dma((4,)),
            dma((8,)),
            dma((4,)),
            dma((12,)),
            dma((2, 6)),
            dma((2, 2)),
            dma((2,)),
        ],
        compiler_params=pltpu.CompilerParams(
            collective_id=0, has_side_effects=True, vmem_limit_bytes=int(53.5 * 1024 * 1024)
        ),
        cost_estimate=pl.CostEstimate(flops=8_000_000_000, bytes_accessed=20_000_000, transcendentals=0),
    )(three_center, screening, density_factor.reshape(-1, B, B), metric_inverse)


def solution(mesh):
    placed = (P(("orb", "aux"), None, None, None), P(("orb", "aux"), None), P("orb", None), P())
    return jax.shard_map(
        on_device, mesh=mesh, in_specs=placed, out_specs=P("orb", None), check_vma=False
    )
```

```python
import jax
import jax.numpy as jnp
from jax import lax
from jax.experimental import pallas as pl
from jax.experimental.pallas import tpu as pltpu
from jax.sharding import PartitionSpec as P

MESH = pl.DeviceIdType.MESH
B = 128
F32 = jnp.float32
BF16 = jnp.bfloat16


def place():
    orb, aux = lax.axis_index("orb"), lax.axis_index("aux")
    return aux % 4, (aux // 4) * 2 + (orb // 2) % 2, orb // 4, orb % 2


def device(x, y, z, c):
    x, y, z = (x + 4) % 4, (y + 4) % 4, (z + 4) % 4
    return (z * 4 + (y % 2) * 2 + c, (y // 2) * 4 + x)


def lanes(parts):
    return jnp.concatenate(parts, axis=1)


def rows(parts):
    return jnp.concatenate(parts, axis=0)


PARTS = ((0, 32), (32, 32), (64, 64))


def kernel(
    t_hbm, scr_ref, d_hbm, j_hbm, o_ref,
    tiles, metric, plain, owned, wants, wants_s, y_out0, y_out1, y_out2, y_in0, y_in1, y_in2,
    z_out0, z_out1, z_out2, z_in0, z_in1, z_in2, factor_t, perm,
    half, mid_x, mid_y, own, foll, fitted, diagonal, coupling, red_in, gathered,
    t_sem, j_sem, d_sem, sib_sem, w_sem, ws_sem, y_sem, z_sem, s1_out, s1_in, s2_out, s2_in, f_sem, r_sem, g_sem,
):
    x, y, z, c = place()
    y_out, y_in = (y_out0, y_out1, y_out2), (y_in0, y_in1, y_in2)
    z_out, z_in = (z_out0, z_out1, z_out2), (z_in0, z_in1, z_in2)

    load_d = pltpu.make_async_copy(d_hbm, plain, d_sem)
    load_d.start()
    load_t = []
    for g in range(2):
        span = pl.ds(g * 64, 64)
        load_t.append(pltpu.make_async_copy(t_hbm.at[:, span], tiles.at[:, span], t_sem.at[g]))
    load_j = pltpu.make_async_copy(j_hbm, metric, j_sem)

    wants[0, z, pl.ds(0, 4), pl.ds(0, 3)] = scr_ref[...]

    plane = [(dx, dy) for dx in range(4) for dy in range(4) if (dx, dy) != (0, 0)]
    above = [(dy, dz) for dy in (1, 3, 0) for dz in (0, 1, 2, 3) if (dy, dz) != (0, 0)]
    barrier = pltpu.get_barrier_semaphore()
    peers = [device(x, y, z, 1 - c), device(x, y, z + 2 * c - 1, 1 - c)]
    peers += [device(x, y + dy, z + dz, c) for dy, dz in above if dz]
    peers += [device(x + dx, y + dy, z, c) for dx, dy in plane]
    for peer in peers:
        pl.semaphore_signal(barrier, inc=1, device_id=peer, device_id_type=MESH)

    r = lax.broadcasted_iota(jnp.int32, (256, 256), 0)
    k = lax.broadcasted_iota(jnp.int32, (256, 256), 1)
    perm[...] = jnp.where((r % 16) * 16 + r // 16 == k, 1.0, 0.0).astype(BF16)
    diagonal[...] = jnp.zeros_like(diagonal)
    coupling[...] = jnp.zeros_like(coupling)

    load_d.wait()
    load_t[0].start()

    @pl.loop(0, 8)
    def _(n):
        for e in range(4):
            owned[c * 32 + n * 4 + e] = plain[n * 4 + e].T

    pl.semaphore_wait(barrier, len(peers))

    def remote(src, dst, send, recv, peer):
        copy = pltpu.make_async_remote_copy(
            src_ref=src, dst_ref=dst, send_sem=send, recv_sem=recv, device_id=peer, device_id_type=MESH
        )
        copy.start()
        return copy

    def done(sem, ref):
        pltpu.make_async_copy(ref, ref, sem).wait()

    for n, (dy, dz) in enumerate(above):
        slot = {0: 0, 1: 1, 3: 2}[dy]
        group = 0 if dy else 1
        remote(wants.at[0, z], wants.at[slot, z], w_sem.at[0, group], w_sem.at[1, group], device(x, y + dy, z + dz, c))
    span = pl.ds(c * 32, 32)
    sibling = remote(owned.at[span], owned.at[span], sib_sem.at[0], sib_sem.at[1], device(x, y, z, 1 - c))
    others, column = pl.ds(1, 2), pl.ds(0, 3)
    done(w_sem.at[1, 0], wants.at[others])
    others_s = pltpu.make_async_copy(wants.at[others], wants_s.at[others], ws_sem.at[0])
    others_s.start()
    done(w_sem.at[1, 1], wants.at[0, column])
    column_s = pltpu.make_async_copy(wants.at[0], wants_s.at[0], ws_sem.at[1])
    column_s.start()
    sibling.wait_recv()
    others_s.wait()

    first = (z * 4 + (y % 2) * 2) * 32

    def pick(column, zz, slot, part):
        block = wants_s[column, zz, slot, 1] - first
        inside = (block >= 0) & (block < 64)
        start, count = PARTS[part]
        found = owned[jnp.clip(block, 0, 63), pl.ds(start, count), :]
        return jnp.where(inside, found, jnp.zeros_like(found))

    for part in range(3):
        for way in range(2):
            @pl.loop(0, 4, unroll=True)
            def _(zz):
                for sub in range(2):
                    y_out[part][way, zz, sub] = pick(2 - way, zz, way * 2 + sub, part)

            remote(
                y_out[part].at[way], y_in[part].at[way], y_sem.at[0, part], y_sem.at[1, part],
                device(x, y + 1 - 2 * way, z, c),
            )
    column_s.wait()
    load_t[1].start()
    load_j.start()

    def along_z(part):
        done(y_sem.at[1, part], y_in[part])
        for way in range(2):
            @pl.loop(0, 4, unroll=True)
            def _(zz):
                for sub in range(2):
                    z_out[part][zz, way * 2 + sub] = pick(0, zz, way * 2 + sub, part) + y_in[part][way, zz, sub]

        for dz in (2, 1, 3):
            remote(
                z_out[part].at[(z + dz) % 4], z_in[part].at[dz - 1], z_sem.at[0, part], z_sem.at[1, part],
                device(x, y, z + dz, c),
            )

    def arrived(part):
        done(z_sem.at[1, part], z_in[part])
        start, count = PARTS[part]
        for slot in range(4):
            block = z_out[part][z, slot]
            for dz in range(3):
                block = block + z_in[part][dz, slot]
            factor_t[pl.ds(start, count), pl.ds(slot * B, B)] = block

    def transform(part, low, high):
        start, count = PARTS[part]

        @pl.loop(low, high)
        def _(g):
            made = []
            for pair in range(8):
                m = g * 16 + pair * 2
                right = rows([lanes([tiles[t, m], tiles[t, m + 1]]) for t in range(4)])
                out = jnp.dot(
                    factor_t[pl.ds(start, count), :], right, preferred_element_type=F32
                ).astype(BF16)
                made += [out[:, :B], out[:, B:]]
            for group in range(0, count // 16, 2):
                stack = lanes([rows([one[(group + e) * 16:(group + e + 1) * 16] for one in made]) for e in range(2)])
                turned = jnp.dot(perm[...], stack, preferred_element_type=F32).astype(BF16)
                for e in range(2):
                    for i in range(16):
                        half[start + (group + e) * 16 + i, pl.ds(pl.multiple_of(g * 16, 16), 16), :] = turned[
                            i * 16:(i + 1) * 16, e * B:(e + 1) * B
                        ]

    def cut(h):
        return {None: pl.ds(0, B), 0: pl.ds(0, 64), 1: pl.ds(64, 64), 2: pl.ds(0, 32), 3: pl.ds(32, 32), 4: pl.ds(64, 32), 5: pl.ds(96, 32)}[h]

    def piece(h):
        return {None: 0, 0: 0, 4: 1, 5: 2}[h]

    def first_hop(chunk, d, h=None):
        n, odd, ms = chunk // 2, chunk % 2, cut(h)
        at = y if odd else x
        land = mid_y.at[n, y // 2, y % 2, :, ms] if odd else mid_x.at[n, x, :, ms]
        source = half.at[pl.ds(chunk * 16 + (at + d) % 4 * 4, 4), ms]
        if d:
            peer = device(x, y + d, z, c) if odd else device(x + d, y, z, c)
            remote(source, land, s1_out.at[n], s1_in.at[chunk], peer)
        else:
            pltpu.make_async_copy(source, land, s1_in.at[chunk]).start()

    def second_hop(chunk, d, h=None):
        n, odd, ms = chunk // 2, chunk % 2, cut(h)
        into = chunk + 2 * piece(h)
        there = ((x if odd else y) + d) % 4
        land = own.at[chunk, :, :, x, ms] if odd else own.at[chunk, y // 2, y % 2, :, ms]
        source = mid_y.at[n, :, :, there, ms] if odd else mid_x.at[n, :, there, ms]
        if d:
            peer = device(x + d, y, z, c) if odd else device(x, y + d, z, c)
            remote(source, land, s2_out.at[n], s2_in.at[into], peer)
        else:
            pltpu.make_async_copy(source, land, s2_in.at[into]).start()

    def follow(chunk, h=None):
        ms, sem = cut(h), chunk // 2 + piece(h)
        remote(
            own.at[chunk, :, c, :, ms], foll.at[chunk, 1, :, :, ms], f_sem.at[0, sem], f_sem.at[1, sem],
            device(x, y, z - (1 - c), 1 - c),
        )
        remote(
            own.at[chunk, :, 1 - c, :, ms], foll.at[chunk, 0, :, :, ms], f_sem.at[0, sem], f_sem.at[1, sem],
            device(x, y, z, 1 - c),
        )

    def first_done(pair):
        done(s1_in.at[pair * 2], mid_x.at[pair])
        done(s1_in.at[pair * 2 + 1], mid_y.at[pair])

    def second_done(pair, h=None):
        for e in range(2):
            done(s2_in.at[pair * 2 + e + 2 * piece(h)], own.at[0, :, :, :, cut(h)])
            follow(pair * 2 + e, h)

    def follow_done(pair, h=None):
        done(f_sem.at[1, pair + piece(h)], foll.at[pl.ds(0, 2), :, :, :, cut(h)])

    def both(hop, pair, h=None):
        for d in (1, 3, 2, 0):
            for e in range(2):
                hop(pair * 2 + e, d, h)

    def own_rows(chunk, s):
        return lanes([own[chunk, g, s, e] for g in range(2) for e in range(4)])

    def foll_rows(chunk, s):
        return lanes([foll[chunk, s, g, e] for g in range(2) for e in range(4)])

    def across(left, right):
        return lax.dot_general(left, right, (((1,), (1,)), ((), ())), preferred_element_type=F32)

    def with_itself(pair):
        for e in range(2):
            chunk = pair * 2 + e
            stack = rows([own_rows(chunk, s) for s in range(2)])
            fitted[pair % 2, e] = jnp.dot(stack, metric[...], preferred_element_type=F32).astype(BF16)
            for s in range(2):
                diagonal[s] += across(fitted[pair % 2, e, pl.ds(s * B, B), :], own_rows(chunk, s))

    def with_next(pair):
        for e in range(2):
            for s in range(2):
                coupling[s] += across(fitted[pair % 2, e, pl.ds(s * B, B), :], foll_rows(pair * 2 + e, s))

    along_z(0)
    along_z(1)
    arrived(0)
    load_t[0].wait()
    transform(0, 0, 2)
    both(first_hop, 0, 2)
    along_z(2)
    transform(0, 2, 4)
    both(first_hop, 0, 3)
    load_t[1].wait()
    transform(0, 4, 8)
    both(first_hop, 0, 1)
    arrived(1)
    transform(1, 0, 4)
    both(first_hop, 1, 0)
    transform(1, 4, 6)
    first_done(0)
    both(second_hop, 0)
    transform(1, 6, 8)
    both(first_hop, 1, 1)
    arrived(2)
    transform(2, 0, 4)
    both(first_hop, 2, 0)
    first_done(1)
    both(second_hop, 1)
    transform(2, 4, 8)
    both(first_hop, 2, 1)
    both(first_hop, 3)
    load_j.wait()
    second_done(0)
    first_done(2)
    both(second_hop, 2)
    with_itself(0)
    second_done(1)
    first_done(3)
    for h in (0, 4, 5):
        both(second_hop, 3, h)
    with_itself(1)
    follow_done(0)
    with_next(0)
    follow_done(1)
    with_next(1)
    second_done(2)
    with_itself(2)
    second_done(3, 0)
    follow_done(2)
    with_next(2)
    for h in (4, 5):
        second_done(3, h)
    with_itself(3)

    def share(xx, yy):
        return pl.ds(pl.multiple_of((((yy + 4) % 4) // 2 * 4 + (xx + 4) % 4) * 16, 16), 16)

    def scatter(which, summand):
        for n, (dx, dy) in enumerate(plane):
            remote(
                summand.at[(y + dy) % 2, share(x + dx, y + dy)], red_in.at[which, n],
                r_sem.at[0, which], r_sem.at[1, which], device(x + dx, y + dy, z, c),
            )

    def collect(which, summand):
        result = summand[y % 2, share(x, y), :]
        done(r_sem.at[1, which], red_in.at[which])
        for n in range(len(plane)):
            result = result + red_in[which, n]
        gathered[share(x, y), pl.ds(which * B, B)] = result.astype(BF16)

    scatter(0, diagonal)
    for h in (0, 4, 5):
        follow_done(3, h)
    with_next(3)
    scatter(1, coupling)
    collect(0, diagonal)
    collect(1, coupling)
    for dx, dy in plane:
        if dy % 2 == 0:
            remote(
                gathered.at[share(x, y)], gathered.at[share(x, y)], g_sem.at[0], g_sem.at[1],
                device(x + dx, y + dy, z, c),
            )

    done(w_sem.at[0, 0], wants.at[others])
    done(w_sem.at[0, 1], wants.at[0, column])
    sibling.wait_send()
    for part in range(3):
        done(y_sem.at[0, part], y_in[part])
        done(z_sem.at[0, part], z_in[part])
    for pair in range(4):
        done(s1_out.at[pair], half.at[pl.ds(0, 24)])
        done(s2_out.at[pair], half.at[pl.ds(0, 24)])
    for pair in range(3):
        done(f_sem.at[0, pair], foll.at[pl.ds(0, 2)])
    for h in (0, 4, 5):
        done(f_sem.at[0, 3 + piece(h)], foll.at[pl.ds(0, 2), :, :, :, cut(h)])
    for which in range(2):
        done(r_sem.at[0, which], red_in.at[which])
    rest = gathered.at[pl.ds(0, 112)]
    done(g_sem.at[0], rest)
    done(g_sem.at[1], rest)
    o_ref[...] = gathered[...]


def on_device(three_center, screening, density_factor, metric_inverse):
    dma = pltpu.SemaphoreType.DMA
    return pl.pallas_call(
        kernel,
        out_shape=jax.ShapeDtypeStruct((B, 2 * B), BF16),
        in_specs=[
            pl.BlockSpec(memory_space=pl.ANY),
            pl.BlockSpec(memory_space=pltpu.VMEM),
            pl.BlockSpec(memory_space=pl.ANY),
            pl.BlockSpec(memory_space=pl.ANY),
        ],
        out_specs=pl.BlockSpec(memory_space=pltpu.VMEM),
        scratch_shapes=[
            pltpu.VMEM((4, B, B, B), BF16),
            pltpu.VMEM((1024, 1024), BF16),
            pltpu.VMEM((32, B, B), BF16),
            pltpu.VMEM((64, B, B), BF16),
            pltpu.VMEM((3, 4, 8, B), jnp.int32),
            pltpu.SMEM((3, 4, 8, B), jnp.int32),
            *[pltpu.VMEM((2, 4, 2, count, B), BF16) for _, count in PARTS],
            *[pltpu.VMEM((2, 4, 2, count, B), BF16) for _, count in PARTS],
            *[pltpu.VMEM((4, 4, count, B), BF16) for _, count in PARTS],
            *[pltpu.VMEM((3, 4, count, B), BF16) for _, count in PARTS],
            pltpu.VMEM((B, 4 * B), BF16),
            pltpu.VMEM((256, 256), BF16),
            pltpu.VMEM((B, B, B), BF16),
            pltpu.VMEM((4, 4, 4, B, B), BF16),
            pltpu.VMEM((4, 2, 2, 4, B, B), BF16),
            pltpu.VMEM((8, 2, 2, 4, B, B), BF16),
            pltpu.VMEM((8, 2, 2, 4, B, B), BF16),
            pltpu.VMEM((2, 2, 2 * B, 1024), BF16),
            pltpu.VMEM((2, B, B), F32),
            pltpu.VMEM((2, B, B), F32),
            pltpu.VMEM((2, 15, 16, B), F32),
            pltpu.VMEM((B, 2 * B), BF16),
            dma((2,)),
            dma,
            dma,
            dma((2,)),
            dma((2, 2)),
            dma((2,)),
            dma((2, 3)),
            dma((2, 3)),
            dma((4,)),
            dma((8,)),
            dma((4,)),
            dma((12,)),
            dma((2, 6)),
            dma((2, 2)),
            dma((2,)),
        ],
        compiler_params=pltpu.CompilerParams(
            collective_id=0, has_side_effects=True, vmem_limit_bytes=int(53.5 * 1024 * 1024)
        ),
        cost_estimate=pl.CostEstimate(flops=8_000_000_000, bytes_accessed=20_000_000, transcendentals=0),
    )(three_center, screening, density_factor.reshape(-1, B, B), metric_inverse)


def solution(mesh):
    placed = (P(("orb", "aux"), None, None, None), P(("orb", "aux"), None), P("orb", None), P())
    return jax.shard_map(
        on_device, mesh=mesh, in_specs=placed, out_specs=P("orb", None), check_vma=False
    )
```

```python
import jax
import jax.numpy as jnp
from jax import lax
from jax.experimental import pallas as pl
from jax.experimental.pallas import tpu as pltpu
from jax.sharding import PartitionSpec as P

MESH = pl.DeviceIdType.MESH
B = 128
F32 = jnp.float32
BF16 = jnp.bfloat16


def place():
    orb, aux = lax.axis_index("orb"), lax.axis_index("aux")
    return aux % 4, (aux // 4) * 2 + (orb // 2) % 2, orb // 4, orb % 2


def device(x, y, z, c):
    x, y, z = (x + 4) % 4, (y + 4) % 4, (z + 4) % 4
    return (z * 4 + (y % 2) * 2 + c, (y // 2) * 4 + x)


def lanes(parts):
    return jnp.concatenate(parts, axis=1)


def rows(parts):
    return jnp.concatenate(parts, axis=0)


PARTS = ((0, 32), (32, 32), (64, 64))


def kernel(
    t_hbm, scr_ref, d_hbm, j_hbm, o_ref,
    tiles, metric, plain, owned, wants, wants_s, y_out0, y_out1, y_out2, y_in0, y_in1, y_in2,
    z_out0, z_out1, z_out2, z_in0, z_in1, z_in2, factor_t, perm,
    half, mid_x, mid_y, own, foll, fitted, diagonal, coupling, red_in, gathered,
    t_sem, j_sem, d_sem, sib_sem, w_sem, ws_sem, y_sem, z_sem, s1_out, s1_in, s2_out, s2_in, f_sem, r_sem, g_sem,
):
    x, y, z, c = place()
    y_out, y_in = (y_out0, y_out1, y_out2), (y_in0, y_in1, y_in2)
    z_out, z_in = (z_out0, z_out1, z_out2), (z_in0, z_in1, z_in2)

    load_d = pltpu.make_async_copy(d_hbm, plain, d_sem)
    load_d.start()
    load_t = []
    for g in range(2):
        span = pl.ds(g * 64, 64)
        load_t.append(pltpu.make_async_copy(t_hbm.at[:, span], tiles.at[:, span], t_sem.at[g]))
    load_j = pltpu.make_async_copy(j_hbm, metric, j_sem)

    wants[0, z, pl.ds(0, 4), pl.ds(0, 3)] = scr_ref[...]

    plane = [(dx, dy) for dx in range(4) for dy in range(4) if (dx, dy) != (0, 0)]
    above = [(dy, dz) for dy in (1, 3, 0) for dz in (0, 1, 2, 3) if (dy, dz) != (0, 0)]
    barrier = pltpu.get_barrier_semaphore()
    peers = [device(x, y, z, 1 - c), device(x, y, z + 2 * c - 1, 1 - c)]
    peers += [device(x, y + dy, z + dz, c) for dy, dz in above if dz]
    peers += [device(x + dx, y + dy, z, c) for dx, dy in plane]
    for peer in peers:
        pl.semaphore_signal(barrier, inc=1, device_id=peer, device_id_type=MESH)

    r = lax.broadcasted_iota(jnp.int32, (256, 256), 0)
    k = lax.broadcasted_iota(jnp.int32, (256, 256), 1)
    perm[...] = jnp.where((r % 16) * 16 + r // 16 == k, 1.0, 0.0).astype(BF16)
    diagonal[...] = jnp.zeros_like(diagonal)
    coupling[...] = jnp.zeros_like(coupling)

    load_d.wait()
    load_t[0].start()

    @pl.loop(0, 8)
    def _(n):
        for e in range(4):
            owned[c * 32 + n * 4 + e] = plain[n * 4 + e].T

    pl.semaphore_wait(barrier, len(peers))

    def remote(src, dst, send, recv, peer):
        copy = pltpu.make_async_remote_copy(
            src_ref=src, dst_ref=dst, send_sem=send, recv_sem=recv, device_id=peer, device_id_type=MESH
        )
        copy.start()
        return copy

    def done(sem, ref):
        pltpu.make_async_copy(ref, ref, sem).wait()

    for n, (dy, dz) in enumerate(above):
        slot = {0: 0, 1: 1, 3: 2}[dy]
        group = 0 if dy else 1
        remote(wants.at[0, z], wants.at[slot, z], w_sem.at[0, group], w_sem.at[1, group], device(x, y + dy, z + dz, c))
    span = pl.ds(c * 32, 32)
    sibling = remote(owned.at[span], owned.at[span], sib_sem.at[0], sib_sem.at[1], device(x, y, z, 1 - c))
    others, column = pl.ds(1, 2), pl.ds(0, 3)
    done(w_sem.at[1, 0], wants.at[others])
    others_s = pltpu.make_async_copy(wants.at[others], wants_s.at[others], ws_sem.at[0])
    others_s.start()
    done(w_sem.at[1, 1], wants.at[0, column])
    column_s = pltpu.make_async_copy(wants.at[0], wants_s.at[0], ws_sem.at[1])
    column_s.start()
    sibling.wait_recv()
    others_s.wait()

    first = (z * 4 + (y % 2) * 2) * 32

    def pick(column, zz, slot, part):
        block = wants_s[column, zz, slot, 1] - first
        inside = (block >= 0) & (block < 64)
        start, count = PARTS[part]
        found = owned[jnp.clip(block, 0, 63), pl.ds(start, count), :]
        return jnp.where(inside, found, jnp.zeros_like(found))

    for part in range(3):
        for way in range(2):
            @pl.loop(0, 4, unroll=True)
            def _(zz):
                for sub in range(2):
                    y_out[part][way, zz, sub] = pick(2 - way, zz, way * 2 + sub, part)

            remote(
                y_out[part].at[way], y_in[part].at[way], y_sem.at[0, part], y_sem.at[1, part],
                device(x, y + 1 - 2 * way, z, c),
            )
    column_s.wait()
    load_t[1].start()
    load_j.start()

    def along_z(part):
        done(y_sem.at[1, part], y_in[part])
        for way in range(2):
            @pl.loop(0, 4, unroll=True)
            def _(zz):
                for sub in range(2):
                    z_out[part][zz, way * 2 + sub] = pick(0, zz, way * 2 + sub, part) + y_in[part][way, zz, sub]

        for dz in (2, 1, 3):
            remote(
                z_out[part].at[(z + dz) % 4], z_in[part].at[dz - 1], z_sem.at[0, part], z_sem.at[1, part],
                device(x, y, z + dz, c),
            )

    def arrived(part):
        done(z_sem.at[1, part], z_in[part])
        start, count = PARTS[part]
        for slot in range(4):
            block = z_out[part][z, slot]
            for dz in range(3):
                block = block + z_in[part][dz, slot]
            factor_t[pl.ds(start, count), pl.ds(slot * B, B)] = block

    def transform(part, low, high):
        start, count = PARTS[part]

        @pl.loop(low, high)
        def _(g):
            made = []
            for pair in range(8):
                m = g * 16 + pair * 2
                right = rows([lanes([tiles[t, m], tiles[t, m + 1]]) for t in range(4)])
                out = jnp.dot(
                    factor_t[pl.ds(start, count), :], right, preferred_element_type=F32
                ).astype(BF16)
                made += [out[:, :B], out[:, B:]]
            for group in range(0, count // 16, 2):
                stack = lanes([rows([one[(group + e) * 16:(group + e + 1) * 16] for one in made]) for e in range(2)])
                turned = jnp.dot(perm[...], stack, preferred_element_type=F32).astype(BF16)
                for e in range(2):
                    for i in range(16):
                        half[start + (group + e) * 16 + i, pl.ds(pl.multiple_of(g * 16, 16), 16), :] = turned[
                            i * 16:(i + 1) * 16, e * B:(e + 1) * B
                        ]

    def cut(h):
        return {None: pl.ds(0, B), 0: pl.ds(0, 64), 1: pl.ds(64, 64), 2: pl.ds(0, 32), 3: pl.ds(32, 32), 4: pl.ds(64, 32), 5: pl.ds(96, 32)}[h]

    def piece(h):
        return {None: 0, 0: 0, 4: 1, 5: 2, 1: 4}[h]

    def first_hop(chunk, d, h=None):
        n, odd, ms = chunk // 2, chunk % 2, cut(h)
        at = y if odd else x
        land = mid_y.at[n, y // 2, y % 2, :, ms] if odd else mid_x.at[n, x, :, ms]
        source = half.at[pl.ds(chunk * 16 + (at + d) % 4 * 4, 4), ms]
        if d:
            peer = device(x, y + d, z, c) if odd else device(x + d, y, z, c)
            remote(source, land, s1_out.at[n], s1_in.at[chunk], peer)
        else:
            pltpu.make_async_copy(source, land, s1_in.at[chunk]).start()

    def second_hop(chunk, d, h=None):
        n, odd, ms = chunk // 2, chunk % 2, cut(h)
        into = chunk + 2 * piece(h)
        there = ((x if odd else y) + d) % 4
        land = own.at[chunk, :, :, x, ms] if odd else own.at[chunk, y // 2, y % 2, :, ms]
        source = mid_y.at[n, :, :, there, ms] if odd else mid_x.at[n, :, there, ms]
        if d:
            peer = device(x + d, y, z, c) if odd else device(x, y + d, z, c)
            remote(source, land, s2_out.at[n], s2_in.at[into], peer)
        else:
            pltpu.make_async_copy(source, land, s2_in.at[into]).start()

    def follow(chunk, h=None):
        ms, sem = cut(h), chunk // 2 + piece(h)
        remote(
            own.at[chunk, :, c, :, ms], foll.at[chunk, 1, :, :, ms], f_sem.at[0, sem], f_sem.at[1, sem],
            device(x, y, z - (1 - c), 1 - c),
        )
        remote(
            own.at[chunk, :, 1 - c, :, ms], foll.at[chunk, 0, :, :, ms], f_sem.at[0, sem], f_sem.at[1, sem],
            device(x, y, z, 1 - c),
        )

    def first_done(pair):
        done(s1_in.at[pair * 2], mid_x.at[pair])
        done(s1_in.at[pair * 2 + 1], mid_y.at[pair])

    def second_done(pair, h=None):
        for e in range(2):
            done(s2_in.at[pair * 2 + e + 2 * piece(h)], own.at[0, :, :, :, cut(h)])
            follow(pair * 2 + e, h)

    def follow_done(pair, h=None):
        done(f_sem.at[1, pair + piece(h)], foll.at[pl.ds(0, 2), :, :, :, cut(h)])

    def both(hop, pair, h=None):
        for d in (1, 3, 2, 0):
            for e in range(2):
                hop(pair * 2 + e, d, h)

    def own_rows(chunk, s):
        return lanes([own[chunk, g, s, e] for g in range(2) for e in range(4)])

    def foll_rows(chunk, s):
        return lanes([foll[chunk, s, g, e] for g in range(2) for e in range(4)])

    def across(left, right):
        return lax.dot_general(left, right, (((1,), (1,)), ((), ())), preferred_element_type=F32)

    def with_itself(pair):
        for e in range(2):
            chunk = pair * 2 + e
            stack = rows([own_rows(chunk, s) for s in range(2)])
            fitted[pair % 2, e] = jnp.dot(stack, metric[...], preferred_element_type=F32).astype(BF16)
            for s in range(2):
                diagonal[s] += across(fitted[pair % 2, e, pl.ds(s * B, B), :], own_rows(chunk, s))

    def with_next(pair):
        for e in range(2):
            for s in range(2):
                coupling[s] += across(fitted[pair % 2, e, pl.ds(s * B, B), :], foll_rows(pair * 2 + e, s))

    along_z(0)
    along_z(1)
    arrived(0)
    load_t[0].wait()
    transform(0, 0, 2)
    both(first_hop, 0, 2)
    along_z(2)
    transform(0, 2, 4)
    both(first_hop, 0, 3)
    load_t[1].wait()
    transform(0, 4, 8)
    both(first_hop, 0, 1)
    arrived(1)
    transform(1, 0, 4)
    both(first_hop, 1, 0)
    transform(1, 4, 6)
    first_done(0)
    both(second_hop, 0)
    transform(1, 6, 8)
    both(first_hop, 1, 1)
    arrived(2)
    transform(2, 0, 4)
    both(first_hop, 2, 0)
    first_done(1)
    both(second_hop, 1)
    transform(2, 4, 8)
    both(first_hop, 2, 1)
    both(first_hop, 3)
    load_j.wait()
    second_done(0)
    first_done(2)
    both(second_hop, 2, 0)
    both(second_hop, 2, 1)
    with_itself(0)
    second_done(1)
    first_done(3)
    for h in (0, 4, 5):
        both(second_hop, 3, h)
    with_itself(1)
    follow_done(0)
    with_next(0)
    follow_done(1)
    with_next(1)
    second_done(2, 0)
    second_done(2, 1)
    with_itself(2)
    second_done(3, 0)
    follow_done(2, 0)
    follow_done(2, 1)
    with_next(2)
    for h in (4, 5):
        second_done(3, h)
    with_itself(3)

    def share(xx, yy):
        return pl.ds(pl.multiple_of((((yy + 4) % 4) // 2 * 4 + (xx + 4) % 4) * 16, 16), 16)

    def scatter(which, summand):
        for n, (dx, dy) in enumerate(plane):
            remote(
                summand.at[(y + dy) % 2, share(x + dx, y + dy)], red_in.at[which, n],
                r_sem.at[0, which], r_sem.at[1, which], device(x + dx, y + dy, z, c),
            )

    def collect(which, summand):
        result = summand[y % 2, share(x, y), :]
        done(r_sem.at[1, which], red_in.at[which])
        for n in range(len(plane)):
            result = result + red_in[which, n]
        gathered[share(x, y), pl.ds(which * B, B)] = result.astype(BF16)

    scatter(0, diagonal)
    for h in (0, 4, 5):
        follow_done(3, h)
    with_next(3)
    scatter(1, coupling)
    collect(0, diagonal)
    collect(1, coupling)
    for dx, dy in plane:
        if dy % 2 == 0:
            remote(
                gathered.at[share(x, y)], gathered.at[share(x, y)], g_sem.at[0], g_sem.at[1],
                device(x + dx, y + dy, z, c),
            )

    done(w_sem.at[0, 0], wants.at[others])
    done(w_sem.at[0, 1], wants.at[0, column])
    sibling.wait_send()
    for part in range(3):
        done(y_sem.at[0, part], y_in[part])
        done(z_sem.at[0, part], z_in[part])
    for pair in range(4):
        done(s1_out.at[pair], half.at[pl.ds(0, 24)])
        done(s2_out.at[pair], half.at[pl.ds(0, 24)])
    for pair in range(2):
        done(f_sem.at[0, pair], foll.at[pl.ds(0, 2)])
    for h in range(2):
        done(f_sem.at[0, 2 + piece(h)], foll.at[pl.ds(0, 2), :, :, :, cut(h)])
    for h in (0, 4, 5):
        done(f_sem.at[0, 3 + piece(h)], foll.at[pl.ds(0, 2), :, :, :, cut(h)])
    for which in range(2):
        done(r_sem.at[0, which], red_in.at[which])
    rest = gathered.at[pl.ds(0, 112)]
    done(g_sem.at[0], rest)
    done(g_sem.at[1], rest)
    o_ref[...] = gathered[...]


def on_device(three_center, screening, density_factor, metric_inverse):
    dma = pltpu.SemaphoreType.DMA
    return pl.pallas_call(
        kernel,
        out_shape=jax.ShapeDtypeStruct((B, 2 * B), BF16),
        in_specs=[
            pl.BlockSpec(memory_space=pl.ANY),
            pl.BlockSpec(memory_space=pltpu.VMEM),
            pl.BlockSpec(memory_space=pl.ANY),
            pl.BlockSpec(memory_space=pl.ANY),
        ],
        out_specs=pl.BlockSpec(memory_space=pltpu.VMEM),
        scratch_shapes=[
            pltpu.VMEM((4, B, B, B), BF16),
            pltpu.VMEM((1024, 1024), BF16),
            pltpu.VMEM((32, B, B), BF16),
            pltpu.VMEM((64, B, B), BF16),
            pltpu.VMEM((3, 4, 8, B), jnp.int32),
            pltpu.SMEM((3, 4, 8, B), jnp.int32),
            *[pltpu.VMEM((2, 4, 2, count, B), BF16) for _, count in PARTS],
            *[pltpu.VMEM((2, 4, 2, count, B), BF16) for _, count in PARTS],
            *[pltpu.VMEM((4, 4, count, B), BF16) for _, count in PARTS],
            *[pltpu.VMEM((3, 4, count, B), BF16) for _, count in PARTS],
            pltpu.VMEM((B, 4 * B), BF16),
            pltpu.VMEM((256, 256), BF16),
            pltpu.VMEM((B, B, B), BF16),
            pltpu.VMEM((4, 4, 4, B, B), BF16),
            pltpu.VMEM((4, 2, 2, 4, B, B), BF16),
            pltpu.VMEM((8, 2, 2, 4, B, B), BF16),
            pltpu.VMEM((8, 2, 2, 4, B, B), BF16),
            pltpu.VMEM((2, 2, 2 * B, 1024), BF16),
            pltpu.VMEM((2, B, B), F32),
            pltpu.VMEM((2, B, B), F32),
            pltpu.VMEM((2, 15, 16, B), F32),
            pltpu.VMEM((B, 2 * B), BF16),
            dma((2,)),
            dma,
            dma,
            dma((2,)),
            dma((2, 2)),
            dma((2,)),
            dma((2, 3)),
            dma((2, 3)),
            dma((4,)),
            dma((8,)),
            dma((4,)),
            dma((14,)),
            dma((2, 7)),
            dma((2, 2)),
            dma((2,)),
        ],
        compiler_params=pltpu.CompilerParams(
            collective_id=0, has_side_effects=True, vmem_limit_bytes=int(53.5 * 1024 * 1024)
        ),
        cost_estimate=pl.CostEstimate(flops=8_000_000_000, bytes_accessed=20_000_000, transcendentals=0),
    )(three_center, screening, density_factor.reshape(-1, B, B), metric_inverse)


def solution(mesh):
    placed = (P(("orb", "aux"), None, None, None), P(("orb", "aux"), None), P("orb", None), P())
    return jax.shard_map(
        on_device, mesh=mesh, in_specs=placed, out_specs=P("orb", None), check_vma=False
    )
```
